32 devices in a mesh: occ: 8 (over z, y), virt: 4 (over x, core).
Axes of the slice: x: 2, y: 2, z: 4, core: 2. Of those that a mesh axis runs over, the one named last changes fastest.
Arguments:
- integrals: bfloat16 [8, 1024, 1536], P('occ', 'virt'), may hold values from -2 to 2
- occupied_energy: float32 [8], replicated, may hold values from -2 to -0.2
- virtual_energy: float32 [1024], replicated, may hold values from 0.5 to 4
- partner_list: int32 [2, 8], replicated, may hold values from 0 to 7, each once within a row
- tile_lists: int32 [2, 8, 4, 56], P(None, 'occ', 'virt'), may hold values from -1 to 63, as said below
Outputs:
- gradient: float32 [8, 1024, 1536], P('occ', 'virt')
The draws below stay inside these ranges and needn't reach their ends.
Inputs may be any that keep to these rules, and one draw needn't show every extreme that they name: Each row partner_list[k] holds every block number once. In each list tile_lists[k, d, s] the live entries stand first, are distinct, and number from 24 to 56; the rest are -1. For each k and d one slice s holds exactly 56 live entries.
All inputs are finite; a program needn't handle non-finite values.
Results may differ from the reference program's by a relative error of at most 0.0021.
Values may be sent and summed in bfloat16 or wider, within the bound.
No kernel may reach another device: no remote copies, remote signals or barrier semaphores. Data moves between devices by JAX's collectives and lax.ppermute only.
A program may use at most 64 MiB of HBM per device.

```python
import jax
import jax.numpy as jnp
from jax import lax

AUX = 1536
VIRT = 1024
TILE = 64
PAIRINGS = 2
OCC_DEV = 1
BLOCKS = 8
ORBS = 8
SLICES = 4
A_TILES = 4
B_TILES = 16
CAP = 56
LOW = 24


def draw_tile_lists(key, part):
    row_count = PAIRINGS * BLOCKS * SLICES
    tile_total = A_TILES * B_TILES
    counts = jax.random.randint(jax.random.fold_in(key, 11), (PAIRINGS, BLOCKS, SLICES), LOW, CAP + 1)
    fullest = jax.random.randint(jax.random.fold_in(key, 12), (PAIRINGS, BLOCKS, 1), 0, SLICES)
    slices = jnp.arange(SLICES, dtype=jnp.int32)[None, None, :]
    counts = jnp.where(slices == fullest, CAP, counts)
    order_keys = jax.random.split(jax.random.fold_in(key, 13), row_count)
    orders = jax.vmap(lambda one_key: jax.random.permutation(one_key, tile_total))(order_keys)
    chosen = orders[:, :CAP].reshape(PAIRINGS, BLOCKS, SLICES, CAP).astype(jnp.int32)
    places = jnp.arange(CAP, dtype=jnp.int32)
    return jnp.where(places < counts[..., None], chosen, -1).astype(jnp.int32)


def steps_of(stream_key, extent, shards, least, top_value):
    level = 1.0
    for dim, blocks in shards:
        heights = jax.random.uniform(jax.random.fold_in(jax.random.fold_in(stream_key, 6), dim), (blocks,), jnp.float32, least / len(shards), top_value / len(shards))
        level = level * jnp.repeat(jnp.exp(heights), extent[dim] // blocks).reshape((-1,) + (1,) * (len(extent) - 1 - dim))
    return level


def centred(key, extent, width, limit, cuts=(), kind=jnp.bfloat16):
    array = jax.random.normal(key, extent, jnp.float32) * width
    if len(cuts) > 0:
        array = steps_of(key, extent, cuts, -0.22, 0.18) * array
    return jnp.clip(array, min=-limit, max=limit).astype(kind)


def setup_inputs(seed: int = 0) -> dict:
    key_list = jax.random.split(jax.random.key(seed), 6)
    integrals = centred(key_list[0], (ORBS, VIRT, AUX), ((AUX + AUX // 4) ** -0.25), 2.0, ((0, 8), (1, 4)))
    occupied_energy = jnp.clip(jax.random.uniform(key_list[1], (ORBS,), jnp.float32, -2.0, -0.2), -2.0, -0.2)
    virtual_energy = jnp.clip(jax.random.uniform(key_list[2], (VIRT,), jnp.float32, 0.5, 4.0), 0.5, 4.0)
    partner_list = jax.vmap(lambda own: jax.random.permutation(own, BLOCKS))(jax.random.split(key_list[3], PAIRINGS)).reshape((PAIRINGS, BLOCKS)).astype(jnp.int32)
    tile_lists = draw_tile_lists(jax.random.fold_in(key_list[5], 71), 0)
    return {"integrals": integrals, "occupied_energy": occupied_energy, "virtual_energy": virtual_energy, "partner_list": partner_list, "tile_lists": tile_lists}


def tiles_of(source):
    orbitals, row_count, aux_width = source.shape
    tile_count = row_count // TILE
    shaped = source.reshape(orbitals, tile_count, TILE, aux_width)
    return shaped.transpose(1, 0, 2, 3).reshape(tile_count, orbitals * TILE, aux_width)


def reference(integrals, occupied_energy, virtual_energy, partner_list, tile_lists):
    orbitals = OCC_DEV
    energy_rows = virtual_energy.reshape(B_TILES, TILE)

    def one_block(block_id):
        start = (block_id * orbitals).astype(jnp.int32)
        own_tiles = tiles_of(lax.dynamic_slice_in_dim(integrals, start, orbitals, 0))
        own_energy = lax.dynamic_slice_in_dim(occupied_energy, start, orbitals, 0)
        totals = jnp.zeros((B_TILES, orbitals * TILE, AUX), jnp.float32)
        for pairing in range(PAIRINGS):
            partner_start = (partner_list[pairing, block_id] * orbitals).astype(jnp.int32)
            partner_tiles = tiles_of(lax.dynamic_slice_in_dim(integrals, partner_start, orbitals, 0))
            partner_energy = lax.dynamic_slice_in_dim(occupied_energy, partner_start, orbitals, 0)
            for slice_id in range(SLICES):
                entries = tile_lists[pairing, block_id, slice_id]
                in_use = entries >= 0
                clamped = jnp.maximum(entries, 0)
                a_tile = (slice_id * A_TILES + clamped // B_TILES).astype(jnp.int32)
                c_tile = (clamped % B_TILES).astype(jnp.int32)
                own_rows = own_tiles[a_tile].astype(jnp.float32)
                partner_rows = partner_tiles[c_tile].astype(jnp.float32)
                scores = jnp.einsum("gxp,gyp->gxy", own_rows, partner_rows)
                gap_left = (energy_rows[a_tile][:, None, :] - own_energy[None, :, None]).reshape(CAP, orbitals * TILE)
                gap_right = (energy_rows[c_tile][:, None, :] - partner_energy[None, :, None]).reshape(CAP, orbitals * TILE)
                ratio = scores / (gap_left[:, :, None] + gap_right[:, None, :])
                amplitude = jnp.where(in_use[:, None, None], ratio, jnp.zeros_like(ratio))
                amplitude = lax.optimization_barrier(amplitude.astype(jnp.bfloat16)).astype(jnp.float32)
                contrib = jnp.einsum("gxy,gyp->gxp", amplitude, partner_rows)
                totals = totals.at[a_tile].add(contrib)
        shaped = totals.reshape(B_TILES, orbitals, TILE, AUX).transpose(1, 0, 2, 3)
        return shaped.reshape(orbitals, VIRT, AUX)

    block_ids = jnp.arange(BLOCKS, dtype=jnp.int32)
    return lax.map(one_block, block_ids).reshape(ORBS, VIRT, AUX)
```

```python
import jax
import jax.numpy as jnp
from jax import lax
from jax.experimental import pallas as pl
from jax.experimental.pallas import tpu as pltpu
from jax.sharding import PartitionSpec as P

TILE = 64
CHUNKS = 4


def xor_pairs(count, mask):
    return [(i, i ^ mask) for i in range(count)]


def listed_weights(entries, a_count, b_count, left_gap, right_gap, slice_order):
    pair_ids = jnp.arange(a_count * b_count, dtype=jnp.int32)
    listed = jnp.any(entries[:, :, None] == pair_ids[None, None, :], axis=1)
    pairings = entries.shape[0]
    slices = slice_order.shape[0]
    listed = listed.reshape(pairings, a_count, slices, b_count // slices)
    listed = jnp.take(listed, slice_order, axis=2)
    listed = jnp.repeat(jnp.repeat(listed, TILE, axis=1), TILE, axis=3)
    right = jnp.take(right_gap, slice_order, axis=1)
    gap = left_gap[None, :, None, None] + right[:, None, :, :]
    return jnp.where(listed, 1.0 / gap, 0.0)


def part_kernel(own_ref, weight_ref, *refs, first):
    if first:
        *row_refs, out_ref = refs
    else:
        *row_refs, total_ref, out_ref = refs
    own = own_ref[...]
    aux = own.shape[-1]
    rows = jnp.concatenate([r[...].reshape(-1, aux) for r in row_refs], axis=0)
    scores = lax.dot_general(own, rows, (((1,), (1,)), ((), ())), preferred_element_type=jnp.float32)
    amplitude = (scores * weight_ref[...]).astype(jnp.bfloat16)
    part = jnp.dot(amplitude, rows, preferred_element_type=jnp.float32)
    if first:
        out_ref[...] = part
    else:
        out_ref[...] = total_ref[...] + part


def add_part(own, weights, rows, total):
    slice_rows, aux = own.shape
    first = total is None
    args = [own, weights, *rows] + ([] if first else [total])
    width = weights.shape[-1]
    nbytes = 2 * (slice_rows + width) * aux + 4 * slice_rows * (width + 2 * aux)
    return pl.pallas_call(
        lambda *refs: part_kernel(*refs, first=first),
        out_shape=jax.ShapeDtypeStruct((slice_rows, aux), jnp.float32),
        in_specs=[pl.BlockSpec(memory_space=pltpu.VMEM)] * len(args),
        out_specs=pl.BlockSpec(memory_space=pltpu.VMEM),
        input_output_aliases={} if first else {len(args) - 1: 0},
        compiler_params=pltpu.CompilerParams(vmem_limit_bytes=48 * 1024 * 1024),
        cost_estimate=pl.CostEstimate(
            flops=4 * slice_rows * width * aux, bytes_accessed=nbytes, transcendentals=0
        ),
    )(*args)


def body(integrals, occupied_energy, virtual_energy, partner_list, tile_lists):
    orbitals, slice_rows, aux = integrals.shape
    occ_count = lax.axis_size("occ")
    virt_count = lax.axis_size("virt")
    myself = lax.axis_index("occ")
    slice_id = lax.axis_index("virt")
    a_count = slice_rows // TILE
    b_count = virtual_energy.shape[0] // TILE
    pairings = partner_list.shape[0]
    bits = occ_count.bit_length() - 1
    pick_bits = bits // 2
    spread_masks = [1 << (bits - 1)] + [1 << i for i in range(bits - pick_bits - 1)]
    pick_unit = 1 << (bits - pick_bits - 1)
    pick_masks = [pick_unit * i for i in range(1, 1 << pick_bits)]
    pick_all = pick_unit * ((1 << pick_bits) - 1)

    own = integrals.reshape(slice_rows, aux)
    partners = jnp.take(partner_list, myself, axis=1)
    slice_order = slice_id ^ jnp.arange(virt_count, dtype=jnp.int32)
    slice_order = jnp.stack([slice_id ^ m for m in range(virt_count)])
    own_energy = lax.dynamic_index_in_dim(occupied_energy, myself, 0, False)
    left_gap = lax.dynamic_slice_in_dim(virtual_energy, slice_id * slice_rows, slice_rows, 0) - own_energy
    right_gap = virtual_energy.reshape(1, virt_count, slice_rows) - occupied_energy[partners][:, None, None]
    weights = listed_weights(tile_lists[:, 0, 0], a_count, b_count, left_gap, right_gap, slice_order)

    rows = slice_rows // CHUNKS
    total = None
    early = []
    for mask in spread_masks[1:]:
        pass
    own_side = {0: own}
    for mask in spread_masks[1:]:
        for held in list(own_side):
            own_side[held ^ mask] = lax.ppermute(own_side[held], "occ", xor_pairs(occ_count, mask))
    for c in range(CHUNKS):
        lo = c * rows
        held = {m: v[lo : lo + rows] for m, v in own_side.items()}
        side = {spread_masks[0]: lax.ppermute(own[lo : lo + rows], "occ", xor_pairs(occ_count, spread_masks[0]))}
        for mask in spread_masks[1:]:
            for m in list(side):
                side[m ^ mask] = lax.ppermute(side[m], "occ", xor_pairs(occ_count, mask))
        held.update(side)

        def chosen(wanted, held=held):
            rel = (wanted ^ myself) & (occ_count - 1 - pick_all)
            result = held[0]
            for m, v in held.items():
                if m:
                    result = jnp.where(rel == m, v, result)
            return result

        picked = jnp.stack([chosen(partners[k]) for k in range(pairings)])
        for mask in pick_masks:
            there = jnp.take(partner_list, myself ^ mask, axis=1)
            outgoing = jnp.stack([chosen(there[k]) for k in range(pairings)])
            arrived = lax.ppermute(outgoing, "occ", xor_pairs(occ_count, mask))
            differs = ((partners ^ myself) & pick_all) == mask
            picked = jnp.where(differs[:, None, None], arrived, picked)
        slices = {0: picked}
        mask = virt_count // 2
        while mask:
            for m in list(slices):
                slices[m ^ mask] = lax.ppermute(slices[m], "virt", xor_pairs(virt_count, mask))
            mask //= 2
        order = list(range(virt_count))
        w = weights[:, :, :, lo : lo + rows].transpose(1, 2, 0, 3).reshape(slice_rows, -1)
        total = add_part(own, w, [slices[m] for m in order], total)
    return total[None]


def solution(mesh):
    return jax.shard_map(
        body,
        mesh=mesh,
        in_specs=(P("occ", "virt", None), P(), P(), P(), P(None, "occ", "virt", None)),
        out_specs=P("occ", "virt", None),
        check_vma=False,
    )
```

```python
import jax
import jax.numpy as jnp
from jax import lax
from jax.experimental import pallas as pl
from jax.experimental.pallas import tpu as pltpu
from jax.sharding import PartitionSpec as P

TILE = 64
SHARES = (2, 2, 2, 2)
PACE = 2
FL, BY = 10**10, 1
NEAR_FIRST = 1
TAIL = 2
XWAIT = 2
GATE = 0
VMEM = pl.BlockSpec(memory_space=pltpu.VMEM)
SMEM = pl.BlockSpec(memory_space=pltpu.SMEM)
ANY = pl.BlockSpec(memory_space=pl.ANY)


def send(value, axis, mask):
    return lax.ppermute(value, axis, [(i, i ^ mask) for i in range(lax.axis_size(axis))])


def after(value, *earlier):
    return lax.optimization_barrier((value, *earlier))[0] if earlier else value


def turn(x, index, axis):
    size = x.shape[axis]
    step = 1
    while step < size:
        shape = x.shape[:axis] + (size // (2 * step), 2, step) + x.shape[axis + 1 :]
        flipped = jnp.flip(x.reshape(shape), axis + 1).reshape(x.shape)
        x = jnp.where((index & step) != 0, flipped, x)
        step *= 2
    return x


class Chain:
    def __init__(self):
        self.last = []

    def call(self, kernel, smem, arrays, outs, name, waits=()):
        waits = [*self.last, *waits]
        count = len(smem) + len(arrays)

        def run(*refs):
            kernel(*refs[:count], *refs[count + len(waits) :])

        result = pl.pallas_call(
            run,
            out_shape=tuple(outs),
            in_specs=[SMEM] * len(smem) + [VMEM] * len(arrays) + [ANY] * len(waits),
            out_specs=(VMEM,) * len(outs),
            compiler_params=pltpu.CompilerParams(vmem_limit_bytes=40 * 1024 * 1024),
            cost_estimate=pl.CostEstimate(flops=FL, bytes_accessed=BY, transcendentals=0),
            name=name,
        )(*smem, *arrays, *waits)
        self.last = [result[0]]
        return result


def part_kernel(*refs, row_count, added):
    left_ref, gap_ref, table_ref, right_ref, key_ref = refs[:5]
    row_refs = refs[5 : 5 + row_count]
    added_refs = refs[5 + row_count : 5 + row_count + added]
    out_refs = refs[5 + row_count + added :]
    rows = jnp.concatenate([r[...] for r in row_refs], axis=0)
    scores = lax.dot_general(
        left_ref[...], rows, (((1,), (1,)), ((), ())), preferred_element_type=jnp.float32
    )
    key = key_ref[...]
    ids = lax.broadcasted_iota(jnp.int32, (table_ref.shape[1], key.shape[1]), 0)
    one_hot = (ids == key).astype(jnp.float32).astype(jnp.bfloat16)
    listed = jnp.dot(table_ref[...], one_hot, preferred_element_type=jnp.float32)
    gap = gap_ref[...] + right_ref[...]
    amplitude = jnp.where(listed > 0.5, scores / gap, 0.0).astype(jnp.bfloat16)
    part = jnp.dot(amplitude, rows, preferred_element_type=jnp.float32)
    for ref in added_refs:
        part += ref[...]
    at = 0
    for ref in out_refs:
        ref[...] = part[at : at + ref.shape[0]]
        at += ref.shape[0]


def body(integrals, occupied_energy, virtual_energy, partner_list, tile_lists):
    orbitals, slice_rows, aux = integrals.shape
    occ_count = lax.axis_size("occ")
    virt_count = lax.axis_size("virt")
    myself = lax.axis_index("occ")
    slice_id = lax.axis_index("virt")
    a_count = slice_rows // TILE
    b_count = virtual_energy.shape[0] // TILE
    pairings = partner_list.shape[0]
    bits = occ_count.bit_length() - 1
    place_bits = bits // 2
    unit = 1 << (bits - place_bits - 1)
    places = 1 << place_bits
    half = occ_count // 2
    column_masks = [1 << i for i in range(bits - place_bits - 1)]
    place = (myself // unit) % places
    piece = slice_rows // places
    shares = SHARES if piece >= 16 * sum(SHARES) else (1,)
    count = len(shares)
    edges = [piece * sum(shares[:c]) // sum(shares) for c in range(count + 1)]
    spans = list(zip(edges[:-1], edges[1:]))
    x_order = [m for m in range(virt_count) if not m & 1]

    def block(n):
        return jax.ShapeDtypeStruct((n, aux), jnp.bfloat16)

    own = integrals.reshape(slice_rows, aux)
    ids = jnp.stack([myself, place]).astype(jnp.int32)
    chain = Chain()

    def cut(ids_ref, own_ref, *out_refs):
        for m in range(places):
            at = pl.multiple_of((ids_ref[1] ^ m) * piece, piece)
            data = own_ref[pl.ds(at, piece), :]
            out_refs[m][...] = data
            for c, (lo, hi) in enumerate(spans):
                out_refs[places + c * places + m][...] = data[lo:hi]

    cuts = chain.call(cut, [ids], [own], [block(piece)] * places + [block(hi - lo) for lo, hi in spans for _ in range(places)], "cut")
    turned = cuts[:places]

    def start_far(c, *deps):
        return [
            send(after(cuts[places + c * places + m], *deps), "occ", half ^ (m * unit)) for m in range(places)
        ]

    lists = tile_lists[:, 0, 0]
    lists_beside = send(lists, "virt", 1)
    beside = send(own, "virt", 1) if count > TAIL else None
    far = {0: start_far(0)}
    near = []
    for m in range(1, places):
        split = edges[NEAR_FIRST] if count > 1 else piece
        first = send(turned[m][:split], "occ", m * unit)
        near.append([(0, first)])
    own_side = {}
    for mask in column_masks:
        for m in [0, *own_side]:
            mine = own_side[m] if m else after(turned[0], *([lists_beside, beside] if count > TAIL else []))
            own_side[m ^ mask] = send(mine, "occ", mask)
    for c in range(1, min(PACE, count)):
        far[c] = start_far(c)

    partner_energy = jnp.take(occupied_energy, jnp.take(partner_list, myself, axis=1), axis=0)
    own_energy = lax.dynamic_index_in_dim(occupied_energy, myself, 0, False)

    def left_side(entries):
        pair_ids = jnp.arange(a_count * b_count, dtype=jnp.int32)
        listed = jnp.any(entries[:, :, None] == pair_ids[None, None, :], axis=1)
        table = listed.reshape(pairings, a_count, b_count).transpose(1, 0, 2)
        return jnp.repeat(table.reshape(a_count, pairings * b_count), TILE, axis=0).astype(jnp.bfloat16)

    energies = turn(turn(virtual_energy.reshape(virt_count, places, piece), slice_id, 0), place, 1)
    energy_mine = turn(virtual_energy.reshape(virt_count, slice_rows), slice_id, 0)
    table = jnp.concatenate([left_side(lists), left_side(lists_beside)], axis=0)
    gap_left = energy_mine[:2].reshape(-1, 1) - own_energy
    right = energies[:, None] - partner_energy[None, :, None, None]
    virt_at = (slice_id ^ jnp.arange(virt_count, dtype=jnp.int32))[:, None, None]
    place_at = (place ^ jnp.arange(places, dtype=jnp.int32))[None, :, None]
    row = (virt_at * places + place_at) * piece + jnp.arange(piece, dtype=jnp.int32)
    key = jnp.arange(pairings, dtype=jnp.int32)[None, :, None, None] * b_count + row[:, None] // TILE

    def column(x, order, chunks):
        return jnp.concatenate([x[m, :, :, slice(*spans[c])].reshape(1, -1) for c in chunks for m in order], axis=1)

    early = list(range(count - TAIL))
    late = list(range(max(count - TAIL, 0), count))
    full_order = x_order + [m ^ 1 for m in x_order]
    set_last = (gap_left[:slice_rows], table[:slice_rows], column(right, full_order, late), column(key, full_order, late))
    set_early = (gap_left, table, column(right, x_order, early), column(key, x_order, early)) if early else ()

    def add_part(left, sides, row_refs, added, outs, name, waits=()):
        arrays = [left, *sides, *row_refs, *added]

        def kernel(*refs):
            part_kernel(*refs, row_count=len(row_refs), added=len(added))

        shapes = [jax.ShapeDtypeStruct((n, aux), jnp.float32) for n in outs]
        return chain.call(kernel, [], arrays, shapes, name, waits)

    far_masks = [half ^ (m * unit) for m in range(places)]
    near_masks = [m * unit for m in range(1, places)]
    group = near_masks + far_masks
    side, got, local, value, wide = {}, {}, {}, {}, {}

    def near_of(t, m):
        at, value = [(at, v) for at, v in near[m] if at <= spans[t][0]][-1]
        return value, spans[t][0] - at

    def stack_side(t):
        lo, hi = spans[t]
        rows = hi - lo
        nears = [near_of(t, m) for m in range(places - 1)]

        def kernel(*refs):
            *in_refs, out_ref = refs
            for i, ref in enumerate(in_refs):
                at = nears[i][1] if i < len(nears) else 0
                out_ref[i * rows : (i + 1) * rows, :] = ref[at : at + rows, :]

        waits = [*set_last, *set_early] if t == 0 else []
        arrays = [v for v, _ in nears] + far[t]
        out = chain.call(kernel, [], arrays, [block(len(group) * rows)], f"stack{t}", waits)[0]
        if t == 0 and count > 1:
            for m in range(1, places):
                split = edges[NEAR_FIRST]
                near[m - 1].append((split, send(after(turned[m][split:], out), "occ", m * unit)))
        stacked = {0: out}
        for mask in column_masks:
            for m in list(stacked):
                stacked[m ^ mask] = send(stacked[m], "occ", mask)
        side[t] = {col: v for col, v in stacked.items() if col}
        return out

    def choose(t):
        lo, hi = spans[t]
        rows = hi - lo
        sources = [(0, turned[0], lo)]
        sources += [(m, v, lo) for m, v in own_side.items()]
        sources += [(m, *near_of(t, i)) for i, m in enumerate(near_masks)]
        sources += [(m, v, 0) for m, v in zip(far_masks, far[t])]
        arrays = [v for _, v, _ in sources]
        for col, v in side[t].items():
            sources += [(m ^ col, len(arrays), i * rows) for i, m in enumerate(group)]
            arrays.append(v)

        def kernel(ids_ref, partner_ref, *refs):
            in_refs, out_refs = refs[: len(arrays)], refs[len(arrays) :]
            for m in range(places):
                for k in range(pairings):
                    here = partner_ref[k, ids_ref[0] ^ (m * unit)] ^ ids_ref[0]
                    for i, (mask, which, at) in enumerate(sources):
                        ref = in_refs[which] if isinstance(which, int) else in_refs[i]

                        @pl.when(here == mask)
                        def _(ref=ref, at=at, k=k, m=m):
                            out_refs[m][k * rows : (k + 1) * rows, :] = ref[at : at + rows, :]

        waits = wide[t - XWAIT] if t >= XWAIT else []
        outs = chain.call(kernel, [ids, partner_list], arrays, [block(pairings * rows)] * places, f"choose{t}", waits)
        local[t] = outs[0]
        got[t] = [send(outs[m], "occ", m * unit) for m in range(1, places)]
        return outs[0]

    def join(t, waits=()):
        rows = spans[t][1] - spans[t][0]

        def kernel(*refs):
            *in_refs, out_ref = refs
            for m, ref in enumerate(in_refs):
                for k in range(pairings):
                    at = (k * places + m) * rows
                    out_ref[at : at + rows, :] = ref[k * rows : (k + 1) * rows, :]

        value[t] = chain.call(
            kernel, [], [local[t], *got[t]], [block(pairings * places * rows)], f"join{t}", waits
        )[0]
        ready = {0: value[t]}
        mask = virt_count // 2
        while mask > 1:
            for m in list(ready):
                ready[m ^ mask] = send(ready[m], "virt", mask)
            mask //= 2
        wide[t] = [ready[m] for m in x_order]

    added = []
    for t in range(count):
        stack_side(t)
        if GATE == 0 and t + PACE < count:
            far[t + PACE] = start_far(t + PACE, *chain.last)
        if t:
            join(t - 1)
        if GATE == 1 and t + PACE < count:
            far[t + PACE] = start_far(t + PACE, *chain.last)
        choose(t)
        if GATE == 2 and t + PACE < count:
            far[t + PACE] = start_far(t + PACE, *chain.last)
    if early:
        lefts = jnp.concatenate([own, beside], axis=0)
        mine, other = add_part(
            lefts, set_early, [v for c in early for v in wide[c]], [], [slice_rows] * 2, "early"
        )
        added = [mine, send(other, "virt", 1)]
    join(count - 1)
    final = [v for c in late for v in wide[c] + [send(w, "virt", 1) for w in wide[c]]]
    return add_part(own, set_last, final, added, [slice_rows], "last")[0][None]


def solution(mesh):
    return jax.shard_map(
        body,
        mesh=mesh,
        in_specs=(P("occ", "virt", None), P(), P(), P(), P(None, "occ", "virt", None)),
        out_specs=P("occ", "virt", None),
        check_vma=False,
    )
```

```python
import jax
import jax.numpy as jnp
from jax import lax
from jax.experimental import pallas as pl
from jax.experimental.pallas import tpu as pltpu
from jax.sharding import PartitionSpec as P

TILE = 64
SHARES = (2, 2, 2, 2)
FGROUPS = ((0,), (1,), (2,), (3,))
FGATE = {2: "c0", 3: "s2"}
FNEED = {2: "c1", 3: "c2"}
NEAR_FIRST, NGATE = 2, "s1"
BSTART, BNEED = "s0", "j0"
XNEED = "j1"
SETNEED = "s1"
EARLY = 1
TAIL = 2
ORDER = "s"
FL, FK, BY = 10**10, 1, 1
WS, WJ, WC = 10**10, 10**10, 10**10
VMEM = pl.BlockSpec(memory_space=pltpu.VMEM)
SMEM = pl.BlockSpec(memory_space=pltpu.SMEM)
ANY = pl.BlockSpec(memory_space=pl.ANY)


def send(value, axis, mask):
    return lax.ppermute(value, axis, [(i, i ^ mask) for i in range(lax.axis_size(axis))])


def after(value, *earlier):
    return lax.optimization_barrier((value, *earlier))[0] if earlier else value


def turn(x, index, axis):
    size = x.shape[axis]
    step = 1
    while step < size:
        shape = x.shape[:axis] + (size // (2 * step), 2, step) + x.shape[axis + 1 :]
        flipped = jnp.flip(x.reshape(shape), axis + 1).reshape(x.shape)
        x = jnp.where((index & step) != 0, flipped, x)
        step *= 2
    return x


class Chain:
    def __init__(self):
        self.last = []

    def call(self, kernel, smem, arrays, outs, name, waits=(), weight=None):
        waits = [*self.last, *waits]
        count = len(smem) + len(arrays)

        def run(*refs):
            kernel(*refs[:count], *refs[count + len(waits) :])

        result = pl.pallas_call(
            run,
            out_shape=tuple(outs),
            in_specs=[SMEM] * len(smem) + [VMEM] * len(arrays) + [ANY] * len(waits),
            out_specs=(VMEM,) * len(outs),
            compiler_params=pltpu.CompilerParams(vmem_limit_bytes=40 * 1024 * 1024),
            cost_estimate=pl.CostEstimate(flops=weight or FL, bytes_accessed=BY, transcendentals=0),
            name=name,
        )(*smem, *arrays, *waits)
        self.last = [result[0]]
        return result


def part_kernel(*refs, row_count, added):
    left_ref, gap_ref, table_ref, right_ref, key_ref = refs[:5]
    row_refs = refs[5 : 5 + row_count]
    added_refs = refs[5 + row_count : 5 + row_count + added]
    out_refs = refs[5 + row_count + added :]
    rows = jnp.concatenate([r[...] for r in row_refs], axis=0)
    scores = lax.dot_general(
        left_ref[...], rows, (((1,), (1,)), ((), ())), preferred_element_type=jnp.float32
    )
    key = key_ref[...]
    ids = lax.broadcasted_iota(jnp.int32, (table_ref.shape[1], key.shape[1]), 0)
    one_hot = (ids == key).astype(jnp.float32).astype(jnp.bfloat16)
    listed = jnp.dot(table_ref[...], one_hot, preferred_element_type=jnp.float32)
    gap = gap_ref[...] + right_ref[...]
    amplitude = jnp.where(listed > 0.5, scores / gap, 0.0).astype(jnp.bfloat16)
    part = jnp.dot(amplitude, rows, preferred_element_type=jnp.float32)
    for ref in added_refs:
        part += ref[...]
    at = 0
    for ref in out_refs:
        ref[...] = part[at : at + ref.shape[0]]
        at += ref.shape[0]


def body(integrals, occupied_energy, virtual_energy, partner_list, tile_lists):
    orbitals, slice_rows, aux = integrals.shape
    occ_count = lax.axis_size("occ")
    virt_count = lax.axis_size("virt")
    myself = lax.axis_index("occ")
    slice_id = lax.axis_index("virt")
    a_count = slice_rows // TILE
    b_count = virtual_energy.shape[0] // TILE
    pairings = partner_list.shape[0]
    bits = occ_count.bit_length() - 1
    place_bits = bits // 2
    unit = 1 << (bits - place_bits - 1)
    places = 1 << place_bits
    half = occ_count // 2
    column_masks = [1 << i for i in range(bits - place_bits - 1)]
    place = (myself // unit) % places
    piece = slice_rows // places
    shares = SHARES if piece >= 16 * sum(SHARES) else (1,)
    count = len(shares)
    edges = [piece * sum(shares[:c]) // sum(shares) for c in range(count + 1)]
    spans = list(zip(edges[:-1], edges[1:]))
    far_groups = FGROUPS if count == sum(map(len, FGROUPS)) else [(c,) for c in range(count)]
    far_spans = [(edges[g[0]], edges[g[-1] + 1]) for g in far_groups]
    x_order = [m for m in range(virt_count) if not m & 1]

    def block(n):
        return jax.ShapeDtypeStruct((n, aux), jnp.bfloat16)

    own = integrals.reshape(slice_rows, aux)
    ids = jnp.stack([myself, place]).astype(jnp.int32)
    chain = Chain()

    def cut(ids_ref, own_ref, *out_refs):
        for m in range(places):
            at = pl.multiple_of((ids_ref[1] ^ m) * piece, piece)
            data = own_ref[pl.ds(at, piece), :]
            out_refs[m][...] = data
            for c, (lo, hi) in enumerate(far_spans):
                out_refs[places + c * places + m][...] = data[lo:hi]

    cuts = chain.call(cut, [ids], [own], [block(piece)] * places + [block(hi - lo) for lo, hi in far_spans for _ in range(places)], "cut")
    turned = cuts[:places]

    def start_far(c, *deps):
        return [
            send(after(cuts[places + c * places + m], *deps), "occ", half ^ (m * unit)) for m in range(places)
        ]

    lists = tile_lists[:, 0, 0]
    lists_beside = send(lists, "virt", 1)
    far = {0: start_far(0)}
    own_side = {}
    for mask in column_masks:
        for m in [0, *own_side]:
            own_side[m ^ mask] = send(own_side[m] if m else turned[0], "occ", mask)
    near = []
    for m in range(1, places):
        split = edges[min(NEAR_FIRST, count)]
        first = send(turned[m][:split], "occ", m * unit)
        near.append([(0, first)])
    for c in range(1, len(far_groups)):
        if c not in FGATE:
            far[c] = start_far(c)

    partner_energy = jnp.take(occupied_energy, jnp.take(partner_list, myself, axis=1), axis=0)
    own_energy = lax.dynamic_index_in_dim(occupied_energy, myself, 0, False)

    def left_side(entries):
        pair_ids = jnp.arange(a_count * b_count, dtype=jnp.int32)
        listed = jnp.any(entries[:, :, None] == pair_ids[None, None, :], axis=1)
        table = listed.reshape(pairings, a_count, b_count).transpose(1, 0, 2)
        return jnp.repeat(table.reshape(a_count, pairings * b_count), TILE, axis=0).astype(jnp.bfloat16)

    energies = turn(turn(virtual_energy.reshape(virt_count, places, piece), slice_id, 0), place, 1)
    energy_mine = turn(virtual_energy.reshape(virt_count, slice_rows), slice_id, 0)
    table = jnp.concatenate([left_side(lists), left_side(lists_beside)], axis=0)
    gap_left = energy_mine[:2].reshape(-1, 1) - own_energy
    right = energies[:, None] - partner_energy[None, :, None, None]
    virt_at = (slice_id ^ jnp.arange(virt_count, dtype=jnp.int32))[:, None, None]
    place_at = (place ^ jnp.arange(places, dtype=jnp.int32))[None, :, None]
    row = (virt_at * places + place_at) * piece + jnp.arange(piece, dtype=jnp.int32)
    key = jnp.arange(pairings, dtype=jnp.int32)[None, :, None, None] * b_count + row[:, None] // TILE

    def column(x, order, chunks):
        return jnp.concatenate([x[m, :, :, slice(*spans[c])].reshape(1, -1) for c in chunks for m in order], axis=1)

    early = list(range(count - TAIL))
    late = list(range(max(count - TAIL, 0), count))
    full_order = x_order + [m ^ 1 for m in x_order]
    sets = {c: (gap_left[:slice_rows], table[:slice_rows], column(right, full_order, [c]), column(key, full_order, [c])) for c in late}
    if early:
        sets[0] = (gap_left, table, column(right, x_order, early), column(key, x_order, early))

    def add_part(left, sides, row_refs, added, outs, name, waits=()):
        arrays = [left, *sides, *row_refs, *added]

        def kernel(*refs):
            part_kernel(*refs, row_count=len(row_refs), added=len(added))

        shapes = [jax.ShapeDtypeStruct((n, aux), jnp.float32) for n in outs]
        return chain.call(kernel, [], arrays, shapes, name, waits, FK)

    far_masks = [half ^ (m * unit) for m in range(places)]
    near_masks = [m * unit for m in range(1, places)]
    group = near_masks + far_masks
    masks, side, got, local, value, wide = {}, {}, {}, {}, {}, {}

    def needed(kind, t):
        label = f"{kind}{t}"
        found = []
        for g, at in FNEED.items():
            if at == label and g in far:
                found += far[g]
        if BNEED == label and beside is not None:
            found.append(beside)
        if kind == XNEED[0] and t - int(XNEED[1]) in wide:
            found += wide[t - int(XNEED[1])]
        if SETNEED == label:
            found += [v for sides in sets.values() for v in sides]
        return found

    def near_of(t, m):
        at, value = [(at, v) for at, v in near[m] if at <= spans[t][0]][-1]
        return value, spans[t][0] - at

    def far_of(t):
        g = [i for i, chunks in enumerate(far_groups) if t in chunks][0]
        return [(v, spans[t][0] - far_spans[g][0]) for v in far[g]]

    def stack_side(t):
        lo, hi = spans[t]
        rows = hi - lo
        parts = [near_of(t, m) for m in range(places - 1)] + far_of(t)
        masks[t] = list(group)
        def kernel(*refs):
            *in_refs, out_ref = refs
            for i, ref in enumerate(in_refs):
                at = parts[i][1]
                out_ref[i * rows : (i + 1) * rows, :] = ref[at : at + rows, :]

        waits = needed("s", t)
        arrays = [v for v, _ in parts]
        out = chain.call(kernel, [], arrays, [block(len(parts) * rows)], f"stack{t}", waits, WS)[0]
        stacked = {0: out}
        for mask in column_masks:
            for m in list(stacked):
                stacked[m ^ mask] = send(stacked[m], "occ", mask)
        side[t] = {col: v for col, v in stacked.items() if col}

    def choose(t):
        lo, hi = spans[t]
        rows = hi - lo
        sources = [(0, turned[0], lo)]
        sources += [(m, v, lo) for m, v in own_side.items()]
        sources += [(m, *near_of(t, i)) for i, m in enumerate(near_masks)]
        sources += [(m, *v) for m, v in zip(far_masks, far_of(t))]
        arrays = [v for _, v, _ in sources]
        for col, v in side[t].items():
            sources += [(m ^ col, len(arrays), i * rows) for i, m in enumerate(masks[t])]
            arrays.append(v)

        def kernel(ids_ref, partner_ref, *refs):
            in_refs, out_refs = refs[: len(arrays)], refs[len(arrays) :]
            for m in range(places):
                for k in range(pairings):
                    here = partner_ref[k, ids_ref[0] ^ (m * unit)] ^ ids_ref[0]
                    for i, (mask, which, at) in enumerate(sources):
                        ref = in_refs[which] if isinstance(which, int) else in_refs[i]

                        @pl.when(here == mask)
                        def _(ref=ref, at=at, k=k, m=m):
                            out_refs[m][k * rows : (k + 1) * rows, :] = ref[at : at + rows, :]

        waits = needed("c", t)
        outs = chain.call(kernel, [ids, partner_list], arrays, [block(pairings * rows)] * places, f"choose{t}", waits, WC)
        local[t] = outs[0]
        got[t] = [send(outs[m], "occ", m * unit) for m in range(1, places)]
        return outs[0]

    def join(t, waits=()):
        rows = spans[t][1] - spans[t][0]
        waits = needed("j", t)

        def kernel(*refs):
            *in_refs, out_ref = refs
            for m, ref in enumerate(in_refs):
                for k in range(pairings):
                    at = (k * places + m) * rows
                    out_ref[at : at + rows, :] = ref[k * rows : (k + 1) * rows, :]

        value[t] = chain.call(
            kernel, [], [local[t], *got[t]], [block(pairings * places * rows)], f"join{t}", waits, WJ
        )[0]
        ready = {0: value[t]}
        mask = virt_count // 2
        while mask > 1:
            for m in list(ready):
                ready[m ^ mask] = send(ready[m], "virt", mask)
            mask //= 2
        wide[t] = [ready[m] for m in x_order]

    added = []
    def add_early():
        lefts = jnp.concatenate([own, beside], axis=0)
        mine, other = add_part(
            lefts, sets[0], [v for c in early for v in wide[c]], [], [slice_rows] * 2, "early"
        )
        return [mine, send(other, "virt", 1)]

    def full(c):
        return wide[c] + [send(w, "virt", 1) for w in wide[c]]

    def gate(kind, t):
        nonlocal beside
        if BSTART == f"{kind}{t}" and early:
            beside = send(after(own, *chain.last), "virt", 1)
        if NGATE == f"{kind}{t}" and NEAR_FIRST < count:
            split = edges[NEAR_FIRST]
            for m in range(1, places):
                near[m - 1].append((split, send(after(turned[m][split:], *chain.last), "occ", m * unit)))
        for g, at in FGATE.items():
            if at == f"{kind}{t}" and g < len(far_groups):
                far[g] = start_far(g, *chain.last)

    beside = None
    for t in range(count):
        steps = [("s", t)] + [("j", t - 1)] * (t > 0)
        if ORDER[t % len(ORDER)] == "j":
            steps = steps[::-1]
        for kind, c in steps:
            (stack_side if kind == "s" else join)(c)
            gate(kind, c)
        if t == count - 1 and EARLY == 0 and early:
            added = add_early()
        choose(t)
        gate("c", t)
    if early and EARLY == 1:
        added = add_early()
    join(count - 1)
    if early and EARLY == 2:
        added = add_early()
    for c in late:
        added = add_part(own, sets[c], full(c), added, [slice_rows], f"late{c}")
    return added[0][None]


def solution(mesh):
    return jax.shard_map(
        body,
        mesh=mesh,
        in_specs=(P("occ", "virt", None), P(), P(), P(), P(None, "occ", "virt", None)),
        out_specs=P("occ", "virt", None),
        check_vma=False,
    )
```

```python
import jax
import jax.numpy as jnp
from jax import lax
from jax.experimental import pallas as pl
from jax.experimental.pallas import tpu as pltpu
from jax.sharding import PartitionSpec as P

TILE = 64
SHARES = (2, 2, 2, 2)
FGROUPS = ((0,), (1,), (2,), (3,))
FGATE = {1: "s0", 2: "s1", 3: "c1"}
FNEED = {}
NEAR_FIRST, NGATE = 2, "c0"
BSTART, BNEED = "s0", "j0"
XNEED = "j1"
SETNEED = "s0"
EARLY = 2
PGATE = "none"
CGATE = True
PCUTS = (128, 128)
PTYPE = jnp.bfloat16
TAIL = 2
ORDER = "s"
FL, FK, BY = 10**10, 1, 1
FE = 10**10
WS, WJ, WC = 10**10, 10**10, 10**10
VMEM = pl.BlockSpec(memory_space=pltpu.VMEM)
SMEM = pl.BlockSpec(memory_space=pltpu.SMEM)
ANY = pl.BlockSpec(memory_space=pl.ANY)


def send(value, axis, mask):
    return lax.ppermute(value, axis, [(i, i ^ mask) for i in range(lax.axis_size(axis))])


def after(value, *earlier):
    return lax.optimization_barrier((value, *earlier))[0] if earlier else value


def turn(x, index, axis):
    size = x.shape[axis]
    step = 1
    while step < size:
        shape = x.shape[:axis] + (size // (2 * step), 2, step) + x.shape[axis + 1 :]
        flipped = jnp.flip(x.reshape(shape), axis + 1).reshape(x.shape)
        x = jnp.where((index & step) != 0, flipped, x)
        step *= 2
    return x


class Chain:
    def __init__(self):
        self.last = []

    def call(self, kernel, smem, arrays, outs, name, waits=(), weight=None):
        waits = [*self.last, *waits]
        count = len(smem) + len(arrays)

        def run(*refs):
            kernel(*refs[:count], *refs[count + len(waits) :])

        result = pl.pallas_call(
            run,
            out_shape=tuple(outs),
            in_specs=[SMEM] * len(smem) + [VMEM] * len(arrays) + [ANY] * len(waits),
            out_specs=(VMEM,) * len(outs),
            compiler_params=pltpu.CompilerParams(vmem_limit_bytes=40 * 1024 * 1024),
            cost_estimate=pl.CostEstimate(flops=weight or FL, bytes_accessed=BY, transcendentals=0),
            name=name,
        )(*smem, *arrays, *waits)
        self.last = [result[0]]
        return result


def part_kernel(*refs, row_count, added):
    left_ref, gap_ref, table_ref, right_ref, key_ref = refs[:5]
    row_refs = refs[5 : 5 + row_count]
    added_refs = refs[5 + row_count : 5 + row_count + added]
    out_refs = refs[5 + row_count + added :]
    rows = jnp.concatenate([r[...] for r in row_refs], axis=0)
    scores = lax.dot_general(
        left_ref[...], rows, (((1,), (1,)), ((), ())), preferred_element_type=jnp.float32
    )
    key = key_ref[...]
    ids = lax.broadcasted_iota(jnp.int32, (table_ref.shape[1], key.shape[1]), 0)
    one_hot = (ids == key).astype(jnp.float32).astype(jnp.bfloat16)
    listed = jnp.dot(table_ref[...], one_hot, preferred_element_type=jnp.float32)
    gap = gap_ref[...] + right_ref[...]
    amplitude = jnp.where(listed > 0.5, scores / gap, 0.0).astype(jnp.bfloat16)
    part = jnp.dot(amplitude, rows, preferred_element_type=jnp.float32)
    if added_refs:
        part += added_refs[0][...]
        if len(added_refs) > 1:
            part += jnp.concatenate([r[...].astype(jnp.float32) for r in added_refs[1:]], axis=0)
    at = 0
    for ref in out_refs:
        ref[...] = part[at : at + ref.shape[0]].astype(ref.dtype)
        at += ref.shape[0]


def body(integrals, occupied_energy, virtual_energy, partner_list, tile_lists):
    orbitals, slice_rows, aux = integrals.shape
    occ_count = lax.axis_size("occ")
    virt_count = lax.axis_size("virt")
    myself = lax.axis_index("occ")
    slice_id = lax.axis_index("virt")
    a_count = slice_rows // TILE
    b_count = virtual_energy.shape[0] // TILE
    pairings = partner_list.shape[0]
    bits = occ_count.bit_length() - 1
    place_bits = bits // 2
    unit = 1 << (bits - place_bits - 1)
    places = 1 << place_bits
    half = occ_count // 2
    column_masks = [1 << i for i in range(bits - place_bits - 1)]
    place = (myself // unit) % places
    piece = slice_rows // places
    shares = SHARES if piece >= 16 * sum(SHARES) else (1,)
    count = len(shares)
    edges = [piece * sum(shares[:c]) // sum(shares) for c in range(count + 1)]
    spans = list(zip(edges[:-1], edges[1:]))
    far_groups = FGROUPS if count == sum(map(len, FGROUPS)) else [(c,) for c in range(count)]
    far_spans = [(edges[g[0]], edges[g[-1] + 1]) for g in far_groups]
    x_order = [m for m in range(virt_count) if not m & 1]

    def block(n):
        return jax.ShapeDtypeStruct((n, aux), jnp.bfloat16)

    own = integrals.reshape(slice_rows, aux)
    ids = jnp.stack([myself, place]).astype(jnp.int32)
    chain = Chain()

    def cut(ids_ref, own_ref, *out_refs):
        for m in range(places):
            at = pl.multiple_of((ids_ref[1] ^ m) * piece, piece)
            data = own_ref[pl.ds(at, piece), :]
            out_refs[m][...] = data
            for c, (lo, hi) in enumerate(far_spans):
                out_refs[places + c * places + m][...] = data[lo:hi]

    cuts = chain.call(cut, [ids], [own], [block(piece)] * places + [block(hi - lo) for lo, hi in far_spans for _ in range(places)], "cut")
    turned = cuts[:places]

    def start_far(c, *deps):
        return [
            send(after(cuts[places + c * places + m], *deps), "occ", half ^ (m * unit)) for m in range(places)
        ]

    lists = tile_lists[:, 0, 0]
    lists_beside = send(lists, "virt", 1)
    far = {0: start_far(0)}
    own_side = {}
    for mask in column_masks:
        for m in [0, *own_side]:
            own_side[m ^ mask] = send(own_side[m] if m else turned[0], "occ", mask)
    near = []
    for m in range(1, places):
        split = edges[min(NEAR_FIRST, count)]
        first = send(turned[m][:split], "occ", m * unit)
        near.append([(0, first)])
    for c in range(1, len(far_groups)):
        if c not in FGATE:
            far[c] = start_far(c)

    partner_energy = jnp.take(occupied_energy, jnp.take(partner_list, myself, axis=1), axis=0)
    own_energy = lax.dynamic_index_in_dim(occupied_energy, myself, 0, False)

    def left_side(entries):
        pair_ids = jnp.arange(a_count * b_count, dtype=jnp.int32)
        listed = jnp.any(entries[:, :, None] == pair_ids[None, None, :], axis=1)
        table = listed.reshape(pairings, a_count, b_count).transpose(1, 0, 2)
        return jnp.repeat(table.reshape(a_count, pairings * b_count), TILE, axis=0).astype(jnp.bfloat16)

    energies = turn(turn(virtual_energy.reshape(virt_count, places, piece), slice_id, 0), place, 1)
    energy_mine = turn(virtual_energy.reshape(virt_count, slice_rows), slice_id, 0)
    table = jnp.concatenate([left_side(lists), left_side(lists_beside)], axis=0)
    gap_left = energy_mine[:2].reshape(-1, 1) - own_energy
    right = energies[:, None] - partner_energy[None, :, None, None]
    virt_at = (slice_id ^ jnp.arange(virt_count, dtype=jnp.int32))[:, None, None]
    place_at = (place ^ jnp.arange(places, dtype=jnp.int32))[None, :, None]
    row = (virt_at * places + place_at) * piece + jnp.arange(piece, dtype=jnp.int32)
    key = jnp.arange(pairings, dtype=jnp.int32)[None, :, None, None] * b_count + row[:, None] // TILE

    def column(x, order, chunks):
        return jnp.concatenate([x[m, :, :, slice(*spans[c])].reshape(1, -1) for c in chunks for m in order], axis=1)

    early = list(range(count - TAIL))
    late = list(range(max(count - TAIL, 0), count))
    full_order = x_order + [m ^ 1 for m in x_order]
    sets = {c: (gap_left[:slice_rows], table[:slice_rows], column(right, full_order, [c]), column(key, full_order, [c])) for c in late}
    if early:
        sets[0] = (gap_left, table, column(right, x_order, early), column(key, x_order, early))

    def add_part(left, sides, row_refs, added, outs, name, waits=()):
        arrays = [left, *sides, *row_refs, *added]

        def kernel(*refs):
            part_kernel(*refs, row_count=len(row_refs), added=len(added))

        shapes = [jax.ShapeDtypeStruct((n, aux), PTYPE if i else jnp.float32) for i, n in enumerate(outs)]
        return chain.call(kernel, [], arrays, shapes, name, waits, FE if name == "early" else FK)

    far_masks = [half ^ (m * unit) for m in range(places)]
    near_masks = [m * unit for m in range(1, places)]
    group = near_masks + far_masks
    masks, side, got, local, value, wide = {}, {}, {}, {}, {}, {}

    def needed(kind, t):
        label = f"{kind}{t}"
        found = []
        for g, at in FNEED.items():
            if at == label and g in far:
                found += far[g]
        if BNEED == label and beside is not None:
            found.append(beside)
        if kind == XNEED[0] and t - int(XNEED[1]) in wide:
            found += wide[t - int(XNEED[1])]
        if SETNEED == label:
            found += [v for sides in sets.values() for v in sides]
        return found

    def near_of(t, m):
        at, value = [(at, v) for at, v in near[m] if at <= spans[t][0]][-1]
        return value, spans[t][0] - at

    def far_of(t):
        g = [i for i, chunks in enumerate(far_groups) if t in chunks][0]
        return [(v, spans[t][0] - far_spans[g][0]) for v in far[g]]

    def stack_side(t):
        lo, hi = spans[t]
        rows = hi - lo
        parts = [near_of(t, m) for m in range(places - 1)] + far_of(t)
        masks[t] = list(group)
        def kernel(*refs):
            *in_refs, out_ref = refs
            for i, ref in enumerate(in_refs):
                at = parts[i][1]
                out_ref[i * rows : (i + 1) * rows, :] = ref[at : at + rows, :]

        waits = needed("s", t)
        arrays = [v for v, _ in parts]
        out = chain.call(kernel, [], arrays, [block(len(parts) * rows)], f"stack{t}", waits, WS)[0]
        stacked = {0: out}
        for mask in column_masks:
            for m in list(stacked):
                stacked[m ^ mask] = send(stacked[m], "occ", mask)
        side[t] = {col: v for col, v in stacked.items() if col}

    def choose(t):
        lo, hi = spans[t]
        rows = hi - lo
        sources = [(0, turned[0], lo)]
        sources += [(m, v, lo) for m, v in own_side.items()]
        sources += [(m, *near_of(t, i)) for i, m in enumerate(near_masks)]
        sources += [(m, *v) for m, v in zip(far_masks, far_of(t))]
        arrays = [v for _, v, _ in sources]
        for col, v in side[t].items():
            sources += [(m ^ col, len(arrays), i * rows) for i, m in enumerate(masks[t])]
            arrays.append(v)

        def kernel(ids_ref, partner_ref, *refs):
            in_refs, out_refs = refs[: len(arrays)], refs[len(arrays) :]
            for m in range(places):
                for k in range(pairings):
                    here = partner_ref[k, ids_ref[0] ^ (m * unit)] ^ ids_ref[0]
                    for i, (mask, which, at) in enumerate(sources):
                        ref = in_refs[which] if isinstance(which, int) else in_refs[i]

                        @pl.when(here == mask)
                        def _(ref=ref, at=at, k=k, m=m):
                            out_refs[m][k * rows : (k + 1) * rows, :] = ref[at : at + rows, :]

        waits = needed("c", t)
        outs = chain.call(kernel, [ids, partner_list], arrays, [block(pairings * rows)] * places, f"choose{t}", waits, WC)
        local[t] = outs[0]
        got[t] = [send(outs[m], "occ", m * unit) for m in range(1, places)]
        return outs[0]

    def join(t, waits=()):
        rows = spans[t][1] - spans[t][0]
        waits = needed("j", t)

        def kernel(*refs):
            *in_refs, out_ref = refs
            for m, ref in enumerate(in_refs):
                for k in range(pairings):
                    at = (k * places + m) * rows
                    out_ref[at : at + rows, :] = ref[k * rows : (k + 1) * rows, :]

        value[t] = chain.call(
            kernel, [], [local[t], *got[t]], [block(pairings * places * rows)], f"join{t}", waits, WJ
        )[0]
        ready = {0: value[t]}
        mask = virt_count // 2
        while mask > 1:
            for m in list(ready):
                ready[m ^ mask] = send(ready[m], "virt", mask)
            mask //= 2
        wide[t] = [ready[m] for m in x_order]

    added, fulls, held_back = [], {}, []
    def add_early():
        lefts = jnp.concatenate([own, beside], axis=0)
        return add_part(
            lefts, sets[0], [v for c in early for v in wide[c]], [], [slice_rows, *PCUTS], "early"
        )

    def full(c):
        if c not in fulls:
            fulls[c] = wide[c] + [send(after(w, *held_back), "virt", 1) for w in wide[c]]
        return fulls[c]

    def gate(kind, t):
        nonlocal beside
        if BSTART == f"{kind}{t}" and early:
            beside = send(after(own, *chain.last), "virt", 1)
        if NGATE == f"{kind}{t}" and NEAR_FIRST < count:
            split = edges[NEAR_FIRST]
            for m in range(1, places):
                near[m - 1].append((split, send(after(turned[m][split:], *chain.last), "occ", m * unit)))
        for g, at in FGATE.items():
            if at == f"{kind}{t}" and g < len(far_groups):
                far[g] = start_far(g, *chain.last)

    beside = None
    for t in range(count):
        steps = [("s", t)] + [("j", t - 1)] * (t > 0)
        if ORDER[t % len(ORDER)] == "j":
            steps = steps[::-1]
        for kind, c in steps:
            (stack_side if kind == "s" else join)(c)
            gate(kind, c)
        if t == count - 1 and EARLY == 0 and early:
            added = add_early()
        choose(t)
        gate("c", t)
    if early and EARLY == 1:
        added = add_early()
    join(count - 1)
    if early and EARLY == 2:
        added = add_early()
    if early:
        held_back = chain.last if CGATE else []
        mine, *others = added
        if PGATE == "j":
            others = [after(v, *chain.last) for v in others]
        added = [mine] + [send(v, "virt", 1) for v in others]
    for c in late:
        added = add_part(own, sets[c], full(c), added, [slice_rows], f"late{c}")
    return added[0][None]


def solution(mesh):
    return jax.shard_map(
        body,
        mesh=mesh,
        in_specs=(P("occ", "virt", None), P(), P(), P(), P(None, "occ", "virt", None)),
        out_specs=P("occ", "virt", None),
        check_vma=False,
    )
```

```python
import jax
import jax.numpy as jnp
from jax import lax
from jax.experimental import pallas as pl
from jax.experimental.pallas import tpu as pltpu
from jax.sharding import PartitionSpec as P

TILE = 64
SHARES = (2, 2, 2, 2)
FGROUPS = ((0,), (1,), (2,), (3,))
FGATE = {1: "s0", 2: "s1", 3: "c1"}
FNEED = {}
NEAR_FIRST, NGATE = 2, "c0"
BSTART, BNEED = "s0", "j0"
XNEED = "j1"
SETNEED = "s0"
EARLY = 2
PGATE = "none"
CGATE = True
PCUTS = 2
STREAM = 3
PTYPE = jnp.bfloat16
TAIL = 1
ORDER = "s"
FL, FK, BY = 10**10, 1, 1
FE = 10**10
WS, WJ, WC = 10**10, 10**10, 10**10
VMEM = pl.BlockSpec(memory_space=pltpu.VMEM)
SMEM = pl.BlockSpec(memory_space=pltpu.SMEM)
ANY = pl.BlockSpec(memory_space=pl.ANY)


def send(value, axis, mask):
    return lax.ppermute(value, axis, [(i, i ^ mask) for i in range(lax.axis_size(axis))])


def after(value, *earlier):
    return lax.optimization_barrier((value, *earlier))[0] if earlier else value


def turn(x, index, axis):
    size = x.shape[axis]
    step = 1
    while step < size:
        shape = x.shape[:axis] + (size // (2 * step), 2, step) + x.shape[axis + 1 :]
        flipped = jnp.flip(x.reshape(shape), axis + 1).reshape(x.shape)
        x = jnp.where((index & step) != 0, flipped, x)
        step *= 2
    return x


class Chain:
    def __init__(self):
        self.last = []

    def call(self, kernel, smem, arrays, outs, name, waits=(), weight=None, out_spec=VMEM, scratch=()):
        waits = [*self.last, *waits]
        count = len(smem) + len(arrays)

        def run(*refs):
            kernel(*refs[:count], *refs[count + len(waits) :])

        result = pl.pallas_call(
            run,
            out_shape=tuple(outs),
            in_specs=[SMEM] * len(smem) + [VMEM] * len(arrays) + [ANY] * len(waits),
            out_specs=(out_spec,) * len(outs),
            scratch_shapes=list(scratch),
            compiler_params=pltpu.CompilerParams(vmem_limit_bytes=40 * 1024 * 1024),
            cost_estimate=pl.CostEstimate(flops=weight or FL, bytes_accessed=BY, transcendentals=0),
            name=name,
        )(*smem, *arrays, *waits)
        self.last = [result[0]]
        return result


def part_kernel(*refs, row_count, added, stream):
    left_ref, gap_ref, table_ref, right_ref, key_ref = refs[:5]
    row_refs = refs[5 : 5 + row_count]
    added_refs = refs[5 + row_count : 5 + row_count + added]
    out_refs = refs[5 + row_count + added :]
    rows = jnp.concatenate([r[...] for r in row_refs], axis=0)
    scores = lax.dot_general(
        left_ref[...], rows, (((1,), (1,)), ((), ())), preferred_element_type=jnp.float32
    )
    key = key_ref[...]
    ids = lax.broadcasted_iota(jnp.int32, (table_ref.shape[1], key.shape[1]), 0)
    one_hot = (ids == key).astype(jnp.float32).astype(jnp.bfloat16)
    listed = jnp.dot(table_ref[...], one_hot, preferred_element_type=jnp.float32)
    gap = gap_ref[...] + right_ref[...]
    amplitude = jnp.where(listed > 0.5, scores / gap, 0.0).astype(jnp.bfloat16)
    if stream:
        out_ref, hold_ref, sems = out_refs
        width = hold_ref.shape[-1]
        copies = []
        for i in range(hold_ref.shape[0]):
            columns = slice(i * width, (i + 1) * width)
            part = jnp.dot(amplitude, rows[:, columns], preferred_element_type=jnp.float32)
            if added_refs:
                part += added_refs[0][:, columns]
                if len(added_refs) > 1:
                    other = [r[:, columns].astype(jnp.float32) for r in added_refs[1:]]
                    part += jnp.concatenate(other, axis=0)
            hold_ref[i] = part
            copies.append(pltpu.make_async_copy(hold_ref.at[i], out_ref.at[:, columns], sems.at[i]))
            copies[-1].start()
        for copy in copies:
            copy.wait()
        return
    part = jnp.dot(amplitude, rows, preferred_element_type=jnp.float32)
    if added_refs:
        part += added_refs[0][...]
        if len(added_refs) > 1:
            part += jnp.concatenate([r[...].astype(jnp.float32) for r in added_refs[1:]], axis=0)
    at = 0
    for ref in out_refs:
        ref[...] = part[at : at + ref.shape[0]].astype(ref.dtype)
        at += ref.shape[0]


def body(integrals, occupied_energy, virtual_energy, partner_list, tile_lists):
    orbitals, slice_rows, aux = integrals.shape
    occ_count = lax.axis_size("occ")
    virt_count = lax.axis_size("virt")
    myself = lax.axis_index("occ")
    slice_id = lax.axis_index("virt")
    a_count = slice_rows // TILE
    b_count = virtual_energy.shape[0] // TILE
    pairings = partner_list.shape[0]
    bits = occ_count.bit_length() - 1
    place_bits = bits // 2
    unit = 1 << (bits - place_bits - 1)
    places = 1 << place_bits
    half = occ_count // 2
    column_masks = [1 << i for i in range(bits - place_bits - 1)]
    place = (myself // unit) % places
    piece = slice_rows // places
    shares = SHARES if piece >= 16 * sum(SHARES) else (1,)
    count = len(shares)
    edges = [piece * sum(shares[:c]) // sum(shares) for c in range(count + 1)]
    spans = list(zip(edges[:-1], edges[1:]))
    far_groups = FGROUPS if count == sum(map(len, FGROUPS)) else [(c,) for c in range(count)]
    far_spans = [(edges[g[0]], edges[g[-1] + 1]) for g in far_groups]
    x_order = [m for m in range(virt_count) if not m & 1]

    def block(n):
        return jax.ShapeDtypeStruct((n, aux), jnp.bfloat16)

    own = integrals.reshape(slice_rows, aux)
    ids = jnp.stack([myself, place]).astype(jnp.int32)
    chain = Chain()

    def cut(ids_ref, own_ref, *out_refs):
        for m in range(places):
            at = pl.multiple_of((ids_ref[1] ^ m) * piece, piece)
            data = own_ref[pl.ds(at, piece), :]
            out_refs[m][...] = data
            for c, (lo, hi) in enumerate(far_spans):
                out_refs[places + c * places + m][...] = data[lo:hi]

    cuts = chain.call(cut, [ids], [own], [block(piece)] * places + [block(hi - lo) for lo, hi in far_spans for _ in range(places)], "cut")
    turned = cuts[:places]

    def start_far(c, *deps):
        return [
            send(after(cuts[places + c * places + m], *deps), "occ", half ^ (m * unit)) for m in range(places)
        ]

    lists = tile_lists[:, 0, 0]
    lists_beside = send(lists, "virt", 1)
    far = {0: start_far(0)}
    own_side = {}
    for mask in column_masks:
        for m in [0, *own_side]:
            own_side[m ^ mask] = send(own_side[m] if m else turned[0], "occ", mask)
    near = []
    for m in range(1, places):
        split = edges[min(NEAR_FIRST, count)]
        first = send(turned[m][:split], "occ", m * unit)
        near.append([(0, first)])
    for c in range(1, len(far_groups)):
        if c not in FGATE:
            far[c] = start_far(c)

    partner_energy = jnp.take(occupied_energy, jnp.take(partner_list, myself, axis=1), axis=0)
    own_energy = lax.dynamic_index_in_dim(occupied_energy, myself, 0, False)

    def left_side(entries):
        pair_ids = jnp.arange(a_count * b_count, dtype=jnp.int32)
        listed = jnp.any(entries[:, :, None] == pair_ids[None, None, :], axis=1)
        table = listed.reshape(pairings, a_count, b_count).transpose(1, 0, 2)
        return jnp.repeat(table.reshape(a_count, pairings * b_count), TILE, axis=0).astype(jnp.bfloat16)

    energies = turn(turn(virtual_energy.reshape(virt_count, places, piece), slice_id, 0), place, 1)
    energy_mine = turn(virtual_energy.reshape(virt_count, slice_rows), slice_id, 0)
    table = jnp.concatenate([left_side(lists), left_side(lists_beside)], axis=0)
    gap_left = energy_mine[:2].reshape(-1, 1) - own_energy
    right = energies[:, None] - partner_energy[None, :, None, None]
    virt_at = (slice_id ^ jnp.arange(virt_count, dtype=jnp.int32))[:, None, None]
    place_at = (place ^ jnp.arange(places, dtype=jnp.int32))[None, :, None]
    row = (virt_at * places + place_at) * piece + jnp.arange(piece, dtype=jnp.int32)
    key = jnp.arange(pairings, dtype=jnp.int32)[None, :, None, None] * b_count + row[:, None] // TILE

    def column(x, order, chunks):
        return jnp.concatenate([x[m, :, :, slice(*spans[c])].reshape(1, -1) for c in chunks for m in order], axis=1)

    early = list(range(count - TAIL))
    late = list(range(max(count - TAIL, 0), count))
    full_order = x_order + [m ^ 1 for m in x_order]
    sets = {c: (gap_left[:slice_rows], table[:slice_rows], column(right, full_order, [c]), column(key, full_order, [c])) for c in late}
    if early:
        sets[0] = (gap_left, table, column(right, x_order, early), column(key, x_order, early))

    def add_part(left, sides, row_refs, added, outs, name, stream=0):
        arrays = [left, *sides, *row_refs, *added]

        def kernel(*refs):
            part_kernel(*refs, row_count=len(row_refs), added=len(added), stream=stream)

        shapes = [jax.ShapeDtypeStruct((n, aux), PTYPE if i else jnp.float32) for i, n in enumerate(outs)]
        weight = FE if name == "early" else FK
        if stream:
            scratch = [
                pltpu.VMEM((stream, left.shape[0], aux // stream), jnp.float32),
                pltpu.SemaphoreType.DMA((stream,)),
            ]
            return chain.call(kernel, [], arrays, shapes, name, (), weight, ANY, scratch)
        return chain.call(kernel, [], arrays, shapes, name, (), weight)

    far_masks = [half ^ (m * unit) for m in range(places)]
    near_masks = [m * unit for m in range(1, places)]
    group = near_masks + far_masks
    masks, side, got, local, value, wide = {}, {}, {}, {}, {}, {}

    def needed(kind, t):
        label = f"{kind}{t}"
        found = []
        for g, at in FNEED.items():
            if at == label and g in far:
                found += far[g]
        if BNEED == label and beside is not None:
            found.append(beside)
        if kind == XNEED[0] and t - int(XNEED[1]) in wide:
            found += wide[t - int(XNEED[1])]
        if SETNEED == label:
            found += [v for sides in sets.values() for v in sides]
        return found

    def near_of(t, m):
        at, value = [(at, v) for at, v in near[m] if at <= spans[t][0]][-1]
        return value, spans[t][0] - at

    def far_of(t):
        g = [i for i, chunks in enumerate(far_groups) if t in chunks][0]
        return [(v, spans[t][0] - far_spans[g][0]) for v in far[g]]

    def stack_side(t):
        lo, hi = spans[t]
        rows = hi - lo
        parts = [near_of(t, m) for m in range(places - 1)] + far_of(t)
        masks[t] = list(group)
        def kernel(*refs):
            *in_refs, out_ref = refs
            for i, ref in enumerate(in_refs):
                at = parts[i][1]
                out_ref[i * rows : (i + 1) * rows, :] = ref[at : at + rows, :]

        waits = needed("s", t)
        arrays = [v for v, _ in parts]
        out = chain.call(kernel, [], arrays, [block(len(parts) * rows)], f"stack{t}", waits, WS)[0]
        stacked = {0: out}
        for mask in column_masks:
            for m in list(stacked):
                stacked[m ^ mask] = send(stacked[m], "occ", mask)
        side[t] = {col: v for col, v in stacked.items() if col}

    def choose(t):
        lo, hi = spans[t]
        rows = hi - lo
        sources = [(0, turned[0], lo)]
        sources += [(m, v, lo) for m, v in own_side.items()]
        sources += [(m, *near_of(t, i)) for i, m in enumerate(near_masks)]
        sources += [(m, *v) for m, v in zip(far_masks, far_of(t))]
        arrays = [v for _, v, _ in sources]
        for col, v in side[t].items():
            sources += [(m ^ col, len(arrays), i * rows) for i, m in enumerate(masks[t])]
            arrays.append(v)

        def kernel(ids_ref, partner_ref, *refs):
            in_refs, out_refs = refs[: len(arrays)], refs[len(arrays) :]
            for m in range(places):
                for k in range(pairings):
                    here = partner_ref[k, ids_ref[0] ^ (m * unit)] ^ ids_ref[0]
                    for i, (mask, which, at) in enumerate(sources):
                        ref = in_refs[which] if isinstance(which, int) else in_refs[i]

                        @pl.when(here == mask)
                        def _(ref=ref, at=at, k=k, m=m):
                            out_refs[m][k * rows : (k + 1) * rows, :] = ref[at : at + rows, :]

        waits = needed("c", t)
        outs = chain.call(kernel, [ids, partner_list], arrays, [block(pairings * rows)] * places, f"choose{t}", waits, WC)
        local[t] = outs[0]
        got[t] = [send(outs[m], "occ", m * unit) for m in range(1, places)]
        return outs[0]

    def join(t, waits=()):
        rows = spans[t][1] - spans[t][0]
        waits = needed("j", t)

        def kernel(*refs):
            *in_refs, out_ref = refs
            for m, ref in enumerate(in_refs):
                for k in range(pairings):
                    at = (k * places + m) * rows
                    out_ref[at : at + rows, :] = ref[k * rows : (k + 1) * rows, :]

        value[t] = chain.call(
            kernel, [], [local[t], *got[t]], [block(pairings * places * rows)], f"join{t}", waits, WJ
        )[0]
        ready = {0: value[t]}
        mask = virt_count // 2
        while mask > 1:
            for m in list(ready):
                ready[m ^ mask] = send(ready[m], "virt", mask)
            mask //= 2
        wide[t] = [ready[m] for m in x_order]

    added, fulls, held_back = [], {}, []
    def add_early():
        lefts = jnp.concatenate([own, beside], axis=0)
        return add_part(
            lefts, sets[0], [v for c in early for v in wide[c]], [], [slice_rows] + [slice_rows // PCUTS] * PCUTS, "early"
        )

    def full(c):
        if c not in fulls:
            fulls[c] = wide[c] + [send(after(w, *held_back), "virt", 1) for w in wide[c]]
        return fulls[c]

    def gate(kind, t):
        nonlocal beside
        if BSTART == f"{kind}{t}" and early:
            beside = send(after(own, *chain.last), "virt", 1)
        if NGATE == f"{kind}{t}" and NEAR_FIRST < count:
            split = edges[NEAR_FIRST]
            for m in range(1, places):
                near[m - 1].append((split, send(after(turned[m][split:], *chain.last), "occ", m * unit)))
        for g, at in FGATE.items():
            if at == f"{kind}{t}" and g < len(far_groups):
                far[g] = start_far(g, *chain.last)

    beside = None
    for t in range(count):
        steps = [("s", t)] + [("j", t - 1)] * (t > 0)
        if ORDER[t % len(ORDER)] == "j":
            steps = steps[::-1]
        for kind, c in steps:
            (stack_side if kind == "s" else join)(c)
            gate(kind, c)
        if t == count - 1 and EARLY == 0 and early:
            added = add_early()
        choose(t)
        gate("c", t)
    if early and EARLY == 1:
        added = add_early()
    join(count - 1)
    if early and EARLY == 2:
        added = add_early()
    if early:
        held_back = chain.last if CGATE else []
        mine, *others = added
        if PGATE == "j":
            others = [after(v, *chain.last) for v in others]
        added = [mine] + [send(v, "virt", 1) for v in others]
    for c in late:
        stream = STREAM if c == late[-1] else 0
        added = add_part(own, sets[c], full(c), added, [slice_rows], f"late{c}", stream)
    return added[0][None]


def solution(mesh):
    return jax.shard_map(
        body,
        mesh=mesh,
        in_specs=(P("occ", "virt", None), P(), P(), P(), P(None, "occ", "virt", None)),
        out_specs=P("occ", "virt", None),
        check_vma=False,
    )
```

```python
import jax
import jax.numpy as jnp
from jax import lax
from jax.experimental import pallas as pl
from jax.experimental.pallas import tpu as pltpu
from jax.sharding import PartitionSpec as P

TILE = 64
SHARES = (2, 2, 2, 2)
FGROUPS = ((0,), (1,), (2,), (3,))
FGATE = {1: "s0", 2: "s1", 3: "c1"}
FNEED = {}
NEAR_FIRST, NGATE = 2, "c0"
BSTART, BNEED = "s0", "j0"
XNEED = "j1"
SETNEED = "s0"
EARLY = 2
PGATE = "none"
CGATE = True
PCUTS = 2
STREAM = 3
PTYPE = jnp.float32
TAIL = 1
ORDER = "s"
FL, FK, BY = 10**10, 1, 1
FE = 10**10
WS, WJ, WC = 10**10, 10**10, 10**10
VMEM = pl.BlockSpec(memory_space=pltpu.VMEM)
SMEM = pl.BlockSpec(memory_space=pltpu.SMEM)
ANY = pl.BlockSpec(memory_space=pl.ANY)


def send(value, axis, mask):
    return lax.ppermute(value, axis, [(i, i ^ mask) for i in range(lax.axis_size(axis))])


def after(value, *earlier):
    return lax.optimization_barrier((value, *earlier))[0] if earlier else value


def turn(x, index, axis):
    size = x.shape[axis]
    step = 1
    while step < size:
        shape = x.shape[:axis] + (size // (2 * step), 2, step) + x.shape[axis + 1 :]
        flipped = jnp.flip(x.reshape(shape), axis + 1).reshape(x.shape)
        x = jnp.where((index & step) != 0, flipped, x)
        step *= 2
    return x


class Chain:
    def __init__(self):
        self.last = []

    def call(self, kernel, smem, arrays, outs, name, waits=(), weight=None, out_spec=VMEM, scratch=()):
        waits = [*self.last, *waits]
        count = len(smem) + len(arrays)

        def run(*refs):
            kernel(*refs[:count], *refs[count + len(waits) :])

        result = pl.pallas_call(
            run,
            out_shape=tuple(outs),
            in_specs=[SMEM] * len(smem) + [VMEM] * len(arrays) + [ANY] * len(waits),
            out_specs=(out_spec,) * len(outs),
            scratch_shapes=list(scratch),
            compiler_params=pltpu.CompilerParams(vmem_limit_bytes=40 * 1024 * 1024),
            cost_estimate=pl.CostEstimate(flops=weight or FL, bytes_accessed=BY, transcendentals=0),
            name=name,
        )(*smem, *arrays, *waits)
        self.last = [result[0]]
        return result


def part_kernel(*refs, row_count, added, stream):
    left_ref, gap_ref, table_ref, right_ref, key_ref = refs[:5]
    row_refs = refs[5 : 5 + row_count]
    added_refs = refs[5 + row_count : 5 + row_count + added]
    out_refs = refs[5 + row_count + added :]
    rows = jnp.concatenate([r[...] for r in row_refs], axis=0)
    scores = lax.dot_general(
        left_ref[...], rows, (((1,), (1,)), ((), ())), preferred_element_type=jnp.float32
    )
    key = key_ref[...]
    ids = lax.broadcasted_iota(jnp.int32, (table_ref.shape[1], key.shape[1]), 0)
    one_hot = (ids == key).astype(jnp.float32).astype(jnp.bfloat16)
    listed = jnp.dot(table_ref[...], one_hot, preferred_element_type=jnp.float32)
    gap = gap_ref[...] + right_ref[...]
    amplitude = jnp.where(listed > 0.5, scores / gap, 0.0).astype(jnp.bfloat16)
    if stream:
        out_ref, hold_ref, sems = out_refs
        width = hold_ref.shape[-1]
        copies = []
        for i in range(hold_ref.shape[0]):
            columns = slice(i * width, (i + 1) * width)
            part = jnp.dot(amplitude, rows[:, columns], preferred_element_type=jnp.float32)
            if added_refs:
                part += added_refs[0][:, columns]
                if len(added_refs) > 1:
                    other = [r[:, columns].astype(jnp.float32) for r in added_refs[1:]]
                    part += jnp.concatenate(other, axis=0)
            hold_ref[i] = part
            copies.append(pltpu.make_async_copy(hold_ref.at[i], out_ref.at[:, columns], sems.at[i]))
            copies[-1].start()
        for copy in copies:
            copy.wait()
        return
    part = jnp.dot(amplitude, rows, preferred_element_type=jnp.float32)
    if added_refs:
        part += added_refs[0][...]
        if len(added_refs) > 1:
            part += jnp.concatenate([r[...].astype(jnp.float32) for r in added_refs[1:]], axis=0)
    at = 0
    for ref in out_refs:
        ref[...] = part[at : at + ref.shape[0]].astype(ref.dtype)
        at += ref.shape[0]


def body(integrals, occupied_energy, virtual_energy, partner_list, tile_lists):
    orbitals, slice_rows, aux = integrals.shape
    occ_count = lax.axis_size("occ")
    virt_count = lax.axis_size("virt")
    myself = lax.axis_index("occ")
    slice_id = lax.axis_index("virt")
    a_count = slice_rows // TILE
    b_count = virtual_energy.shape[0] // TILE
    pairings = partner_list.shape[0]
    bits = occ_count.bit_length() - 1
    place_bits = bits // 2
    unit = 1 << (bits - place_bits - 1)
    places = 1 << place_bits
    half = occ_count // 2
    column_masks = [1 << i for i in range(bits - place_bits - 1)]
    place = (myself // unit) % places
    piece = slice_rows // places
    shares = SHARES if piece >= 16 * sum(SHARES) else (1,)
    count = len(shares)
    edges = [piece * sum(shares[:c]) // sum(shares) for c in range(count + 1)]
    spans = list(zip(edges[:-1], edges[1:]))
    far_groups = FGROUPS if count == sum(map(len, FGROUPS)) else [(c,) for c in range(count)]
    far_spans = [(edges[g[0]], edges[g[-1] + 1]) for g in far_groups]
    x_order = [m for m in range(virt_count) if not m & 1]

    def block(n):
        return jax.ShapeDtypeStruct((n, aux), jnp.bfloat16)

    own = integrals.reshape(slice_rows, aux)
    ids = jnp.stack([myself, place]).astype(jnp.int32)
    chain = Chain()

    def cut(ids_ref, own_ref, *out_refs):
        for m in range(places):
            at = pl.multiple_of((ids_ref[1] ^ m) * piece, piece)
            data = own_ref[pl.ds(at, piece), :]
            out_refs[m][...] = data
            for c, (lo, hi) in enumerate(far_spans):
                out_refs[places + c * places + m][...] = data[lo:hi]

    cuts = chain.call(cut, [ids], [own], [block(piece)] * places + [block(hi - lo) for lo, hi in far_spans for _ in range(places)], "cut")
    turned = cuts[:places]

    def start_far(c, *deps):
        return [
            send(after(cuts[places + c * places + m], *deps), "occ", half ^ (m * unit)) for m in range(places)
        ]

    lists = tile_lists[:, 0, 0]
    lists_beside = send(lists, "virt", 1)
    far = {0: start_far(0)}
    own_side = {}
    for mask in column_masks:
        for m in [0, *own_side]:
            own_side[m ^ mask] = send(own_side[m] if m else turned[0], "occ", mask)
    near = []
    for m in range(1, places):
        split = edges[min(NEAR_FIRST, count)]
        first = send(turned[m][:split], "occ", m * unit)
        near.append([(0, first)])
    for c in range(1, len(far_groups)):
        if c not in FGATE:
            far[c] = start_far(c)

    partner_energy = jnp.take(occupied_energy, jnp.take(partner_list, myself, axis=1), axis=0)
    own_energy = lax.dynamic_index_in_dim(occupied_energy, myself, 0, False)

    def left_side(entries):
        pair_ids = jnp.arange(a_count * b_count, dtype=jnp.int32)
        listed = jnp.any(entries[:, :, None] == pair_ids[None, None, :], axis=1)
        table = listed.reshape(pairings, a_count, b_count).transpose(1, 0, 2)
        return jnp.repeat(table.reshape(a_count, pairings * b_count), TILE, axis=0).astype(jnp.bfloat16)

    energies = turn(turn(virtual_energy.reshape(virt_count, places, piece), slice_id, 0), place, 1)
    energy_mine = turn(virtual_energy.reshape(virt_count, slice_rows), slice_id, 0)
    table = jnp.concatenate([left_side(lists), left_side(lists_beside)], axis=0)
    gap_left = energy_mine[:2].reshape(-1, 1) - own_energy
    right = energies[:, None] - partner_energy[None, :, None, None]
    virt_at = (slice_id ^ jnp.arange(virt_count, dtype=jnp.int32))[:, None, None]
    place_at = (place ^ jnp.arange(places, dtype=jnp.int32))[None, :, None]
    row = (virt_at * places + place_at) * piece + jnp.arange(piece, dtype=jnp.int32)
    key = jnp.arange(pairings, dtype=jnp.int32)[None, :, None, None] * b_count + row[:, None] // TILE

    def column(x, order, chunks):
        return jnp.concatenate([x[m, :, :, slice(*spans[c])].reshape(1, -1) for c in chunks for m in order], axis=1)

    early = list(range(count - TAIL))
    late = list(range(max(count - TAIL, 0), count))
    full_order = x_order + [m ^ 1 for m in x_order]
    sets = {c: (gap_left[:slice_rows], table[:slice_rows], column(right, full_order, [c]), column(key, full_order, [c])) for c in late}
    if early:
        sets[0] = (gap_left, table, column(right, x_order, early), column(key, x_order, early))

    def add_part(left, sides, row_refs, added, outs, name, stream=0):
        arrays = [left, *sides, *row_refs, *added]

        def kernel(*refs):
            part_kernel(*refs, row_count=len(row_refs), added=len(added), stream=stream)

        shapes = [jax.ShapeDtypeStruct((n, aux), PTYPE if i else jnp.float32) for i, n in enumerate(outs)]
        weight = FE if name == "early" else FK
        if stream:
            scratch = [
                pltpu.VMEM((stream, left.shape[0], aux // stream), jnp.float32),
                pltpu.SemaphoreType.DMA((stream,)),
            ]
            return chain.call(kernel, [], arrays, shapes, name, (), weight, ANY, scratch)
        return chain.call(kernel, [], arrays, shapes, name, (), weight)

    far_masks = [half ^ (m * unit) for m in range(places)]
    near_masks = [m * unit for m in range(1, places)]
    group = near_masks + far_masks
    masks, side, got, local, value, wide = {}, {}, {}, {}, {}, {}

    def needed(kind, t):
        label = f"{kind}{t}"
        found = []
        for g, at in FNEED.items():
            if at == label and g in far:
                found += far[g]
        if BNEED == label and beside is not None:
            found.append(beside)
        if kind == XNEED[0] and t - int(XNEED[1]) in wide:
            found += wide[t - int(XNEED[1])]
        if SETNEED == label:
            found += [v for sides in sets.values() for v in sides]
        return found

    def near_of(t, m):
        at, value = [(at, v) for at, v in near[m] if at <= spans[t][0]][-1]
        return value, spans[t][0] - at

    def far_of(t):
        g = [i for i, chunks in enumerate(far_groups) if t in chunks][0]
        return [(v, spans[t][0] - far_spans[g][0]) for v in far[g]]

    def stack_side(t):
        lo, hi = spans[t]
        rows = hi - lo
        parts = [near_of(t, m) for m in range(places - 1)] + far_of(t)
        masks[t] = list(group)
        def kernel(*refs):
            *in_refs, out_ref = refs
            for i, ref in enumerate(in_refs):
                at = parts[i][1]
                out_ref[i * rows : (i + 1) * rows, :] = ref[at : at + rows, :]

        waits = needed("s", t)
        arrays = [v for v, _ in parts]
        out = chain.call(kernel, [], arrays, [block(len(parts) * rows)], f"stack{t}", waits, WS)[0]
        stacked = {0: out}
        for mask in column_masks:
            for m in list(stacked):
                stacked[m ^ mask] = send(stacked[m], "occ", mask)
        side[t] = {col: v for col, v in stacked.items() if col}

    def choose(t):
        lo, hi = spans[t]
        rows = hi - lo
        sources = [(0, turned[0], lo)]
        sources += [(m, v, lo) for m, v in own_side.items()]
        sources += [(m, *near_of(t, i)) for i, m in enumerate(near_masks)]
        sources += [(m, *v) for m, v in zip(far_masks, far_of(t))]
        arrays = [v for _, v, _ in sources]
        for col, v in side[t].items():
            sources += [(m ^ col, len(arrays), i * rows) for i, m in enumerate(masks[t])]
            arrays.append(v)

        def kernel(ids_ref, partner_ref, *refs):
            in_refs, out_refs = refs[: len(arrays)], refs[len(arrays) :]
            for m in range(places):
                for k in range(pairings):
                    here = partner_ref[k, ids_ref[0] ^ (m * unit)] ^ ids_ref[0]
                    for i, (mask, which, at) in enumerate(sources):
                        ref = in_refs[which] if isinstance(which, int) else in_refs[i]

                        @pl.when(here == mask)
                        def _(ref=ref, at=at, k=k, m=m):
                            out_refs[m][k * rows : (k + 1) * rows, :] = ref[at : at + rows, :]

        waits = needed("c", t)
        outs = chain.call(kernel, [ids, partner_list], arrays, [block(pairings * rows)] * places, f"choose{t}", waits, WC)
        local[t] = outs[0]
        got[t] = [send(outs[m], "occ", m * unit) for m in range(1, places)]
        return outs[0]

    def join(t, waits=()):
        rows = spans[t][1] - spans[t][0]
        waits = needed("j", t)

        def kernel(*refs):
            *in_refs, out_ref = refs
            for m, ref in enumerate(in_refs):
                for k in range(pairings):
                    at = (k * places + m) * rows
                    out_ref[at : at + rows, :] = ref[k * rows : (k + 1) * rows, :]

        value[t] = chain.call(
            kernel, [], [local[t], *got[t]], [block(pairings * places * rows)], f"join{t}", waits, WJ
        )[0]
        ready = {0: value[t]}
        mask = virt_count // 2
        while mask > 1:
            for m in list(ready):
                ready[m ^ mask] = send(ready[m], "virt", mask)
            mask //= 2
        wide[t] = [ready[m] for m in x_order]

    added, fulls, held_back = [], {}, []
    def add_early():
        lefts = jnp.concatenate([own, beside], axis=0)
        return add_part(
            lefts, sets[0], [v for c in early for v in wide[c]], [], [slice_rows] + [slice_rows // PCUTS] * PCUTS, "early"
        )

    def full(c):
        if c not in fulls:
            fulls[c] = wide[c] + [send(after(w, *held_back), "virt", 1) for w in wide[c]]
        return fulls[c]

    def gate(kind, t):
        nonlocal beside
        if BSTART == f"{kind}{t}" and early:
            beside = send(after(own, *chain.last), "virt", 1)
        if NGATE == f"{kind}{t}" and NEAR_FIRST < count:
            split = edges[NEAR_FIRST]
            for m in range(1, places):
                near[m - 1].append((split, send(after(turned[m][split:], *chain.last), "occ", m * unit)))
        for g, at in FGATE.items():
            if at == f"{kind}{t}" and g < len(far_groups):
                far[g] = start_far(g, *chain.last)

    beside = None
    for t in range(count):
        steps = [("s", t)] + [("j", t - 1)] * (t > 0)
        if ORDER[t % len(ORDER)] == "j":
            steps = steps[::-1]
        for kind, c in steps:
            (stack_side if kind == "s" else join)(c)
            gate(kind, c)
        if t == count - 1 and EARLY == 0 and early:
            added = add_early()
        choose(t)
        gate("c", t)
    if early and EARLY == 1:
        added = add_early()
    join(count - 1)
    if early and EARLY == 2:
        added = add_early()
    if early:
        held_back = chain.last if CGATE else []
        mine, *others = added
        if PGATE == "j":
            others = [after(v, *chain.last) for v in others]
        added = [mine] + [send(v, "virt", 1) for v in others]
    for c in late:
        stream = STREAM if c == late[-1] else 0
        added = add_part(own, sets[c], full(c), added, [slice_rows], f"late{c}", stream)
    return added[0][None]


def solution(mesh):
    return jax.shard_map(
        body,
        mesh=mesh,
        in_specs=(P("occ", "virt", None), P(), P(), P(), P(None, "occ", "virt", None)),
        out_specs=P("occ", "virt", None),
        check_vma=False,
    )
```

```python
import jax
import jax.numpy as jnp
from jax import lax
from jax.experimental import pallas as pl
from jax.experimental.pallas import tpu as pltpu
from jax.sharding import PartitionSpec as P

TILE = 64
SHARES = (2, 2, 2, 2)
FGROUPS = ((0,), (1,), (2,), (3,))
FGATE = {1: "s0", 2: "s1", 3: "c1"}
FNEED = {}
NEAR_FIRST, NGATE = 2, "c0"
BSTART, BNEED = "s0", "j0"
XNEED = "j1"
SETNEED = "s0"
EARLY = 2
PGATE = "none"
CGATE = True
PCUTS = 2
STREAM = 3
PTYPE = jnp.float32
TAIL = 1
ORDER = "s"
FL, FK, BY = 10**10, 1, 1
FE = 10**10
WS, WJ, WC = 10**10, 2 * 10**10, 2 * 10**10
VMEM = pl.BlockSpec(memory_space=pltpu.VMEM)
SMEM = pl.BlockSpec(memory_space=pltpu.SMEM)
ANY = pl.BlockSpec(memory_space=pl.ANY)


def send(value, axis, mask):
    return lax.ppermute(value, axis, [(i, i ^ mask) for i in range(lax.axis_size(axis))])


def after(value, *earlier):
    return lax.optimization_barrier((value, *earlier))[0] if earlier else value


def turn(x, index, axis):
    size = x.shape[axis]
    step = 1
    while step < size:
        shape = x.shape[:axis] + (size // (2 * step), 2, step) + x.shape[axis + 1 :]
        flipped = jnp.flip(x.reshape(shape), axis + 1).reshape(x.shape)
        x = jnp.where((index & step) != 0, flipped, x)
        step *= 2
    return x


class Chain:
    def __init__(self):
        self.last = []

    def call(self, kernel, smem, arrays, outs, name, waits=(), weight=None, out_spec=VMEM, scratch=()):
        waits = [*self.last, *waits]
        count = len(smem) + len(arrays)

        def run(*refs):
            kernel(*refs[:count], *refs[count + len(waits) :])

        result = pl.pallas_call(
            run,
            out_shape=tuple(outs),
            in_specs=[SMEM] * len(smem) + [VMEM] * len(arrays) + [ANY] * len(waits),
            out_specs=(out_spec,) * len(outs),
            scratch_shapes=list(scratch),
            compiler_params=pltpu.CompilerParams(vmem_limit_bytes=40 * 1024 * 1024),
            cost_estimate=pl.CostEstimate(flops=weight or FL, bytes_accessed=BY, transcendentals=0),
            name=name,
        )(*smem, *arrays, *waits)
        self.last = [result[0]]
        return result


def part_kernel(*refs, row_count, added, stream):
    left_ref, gap_ref, table_ref, right_ref, key_ref = refs[:5]
    row_refs = refs[5 : 5 + row_count]
    added_refs = refs[5 + row_count : 5 + row_count + added]
    out_refs = refs[5 + row_count + added :]
    rows = jnp.concatenate([r[...] for r in row_refs], axis=0)
    scores = lax.dot_general(
        left_ref[...], rows, (((1,), (1,)), ((), ())), preferred_element_type=jnp.float32
    )
    key = key_ref[...]
    ids = lax.broadcasted_iota(jnp.int32, (table_ref.shape[1], key.shape[1]), 0)
    one_hot = (ids == key).astype(jnp.float32).astype(jnp.bfloat16)
    listed = jnp.dot(table_ref[...], one_hot, preferred_element_type=jnp.float32)
    gap = gap_ref[...] + right_ref[...]
    amplitude = jnp.where(listed > 0.5, scores / gap, 0.0).astype(jnp.bfloat16)
    if stream:
        out_ref, hold_ref, sems = out_refs
        width = hold_ref.shape[-1]
        copies = []
        for i in range(hold_ref.shape[0]):
            columns = slice(i * width, (i + 1) * width)
            part = jnp.dot(amplitude, rows[:, columns], preferred_element_type=jnp.float32)
            if added_refs:
                part += added_refs[0][:, columns]
                if len(added_refs) > 1:
                    other = [r[:, columns].astype(jnp.float32) for r in added_refs[1:]]
                    part += jnp.concatenate(other, axis=0)
            hold_ref[i] = part
            copies.append(pltpu.make_async_copy(hold_ref.at[i], out_ref.at[:, columns], sems.at[i]))
            copies[-1].start()
        for copy in copies:
            copy.wait()
        return
    part = jnp.dot(amplitude, rows, preferred_element_type=jnp.float32)
    if added_refs:
        part += added_refs[0][...]
        if len(added_refs) > 1:
            part += jnp.concatenate([r[...].astype(jnp.float32) for r in added_refs[1:]], axis=0)
    at = 0
    for ref in out_refs:
        ref[...] = part[at : at + ref.shape[0]].astype(ref.dtype)
        at += ref.shape[0]


def body(integrals, occupied_energy, virtual_energy, partner_list, tile_lists):
    orbitals, slice_rows, aux = integrals.shape
    occ_count = lax.axis_size("occ")
    virt_count = lax.axis_size("virt")
    myself = lax.axis_index("occ")
    slice_id = lax.axis_index("virt")
    a_count = slice_rows // TILE
    b_count = virtual_energy.shape[0] // TILE
    pairings = partner_list.shape[0]
    bits = occ_count.bit_length() - 1
    place_bits = bits // 2
    unit = 1 << (bits - place_bits - 1)
    places = 1 << place_bits
    half = occ_count // 2
    column_masks = [1 << i for i in range(bits - place_bits - 1)]
    place = (myself // unit) % places
    piece = slice_rows // places
    shares = SHARES if piece >= 16 * sum(SHARES) else (1,)
    count = len(shares)
    edges = [piece * sum(shares[:c]) // sum(shares) for c in range(count + 1)]
    spans = list(zip(edges[:-1], edges[1:]))
    far_groups = FGROUPS if count == sum(map(len, FGROUPS)) else [(c,) for c in range(count)]
    far_spans = [(edges[g[0]], edges[g[-1] + 1]) for g in far_groups]
    x_order = [m for m in range(virt_count) if not m & 1]

    def block(n):
        return jax.ShapeDtypeStruct((n, aux), jnp.bfloat16)

    own = integrals.reshape(slice_rows, aux)
    ids = jnp.stack([myself, place]).astype(jnp.int32)
    chain = Chain()

    def cut(ids_ref, own_ref, *out_refs):
        for m in range(places):
            at = pl.multiple_of((ids_ref[1] ^ m) * piece, piece)
            data = own_ref[pl.ds(at, piece), :]
            out_refs[m][...] = data
            for c, (lo, hi) in enumerate(far_spans):
                out_refs[places + c * places + m][...] = data[lo:hi]

    cuts = chain.call(cut, [ids], [own], [block(piece)] * places + [block(hi - lo) for lo, hi in far_spans for _ in range(places)], "cut")
    turned = cuts[:places]

    def start_far(c, *deps):
        return [
            send(after(cuts[places + c * places + m], *deps), "occ", half ^ (m * unit)) for m in range(places)
        ]

    lists = tile_lists[:, 0, 0]
    lists_beside = send(lists, "virt", 1)
    far = {0: start_far(0)}
    own_side = {}
    for mask in column_masks:
        for m in [0, *own_side]:
            own_side[m ^ mask] = send(own_side[m] if m else turned[0], "occ", mask)
    near = []
    for m in range(1, places):
        split = edges[min(NEAR_FIRST, count)]
        first = send(turned[m][:split], "occ", m * unit)
        near.append([(0, first)])
    for c in range(1, len(far_groups)):
        if c not in FGATE:
            far[c] = start_far(c)

    partner_energy = jnp.take(occupied_energy, jnp.take(partner_list, myself, axis=1), axis=0)
    own_energy = lax.dynamic_index_in_dim(occupied_energy, myself, 0, False)

    def left_side(entries):
        pair_ids = jnp.arange(a_count * b_count, dtype=jnp.int32)
        listed = jnp.any(entries[:, :, None] == pair_ids[None, None, :], axis=1)
        table = listed.reshape(pairings, a_count, b_count).transpose(1, 0, 2)
        return jnp.repeat(table.reshape(a_count, pairings * b_count), TILE, axis=0).astype(jnp.bfloat16)

    energies = turn(turn(virtual_energy.reshape(virt_count, places, piece), slice_id, 0), place, 1)
    energy_mine = turn(virtual_energy.reshape(virt_count, slice_rows), slice_id, 0)
    table = jnp.concatenate([left_side(lists), left_side(lists_beside)], axis=0)
    gap_left = energy_mine[:2].reshape(-1, 1) - own_energy
    right = energies[:, None] - partner_energy[None, :, None, None]
    virt_at = (slice_id ^ jnp.arange(virt_count, dtype=jnp.int32))[:, None, None]
    place_at = (place ^ jnp.arange(places, dtype=jnp.int32))[None, :, None]
    row = (virt_at * places + place_at) * piece + jnp.arange(piece, dtype=jnp.int32)
    key = jnp.arange(pairings, dtype=jnp.int32)[None, :, None, None] * b_count + row[:, None] // TILE

    def column(x, order, chunks):
        return jnp.concatenate([x[m, :, :, slice(*spans[c])].reshape(1, -1) for c in chunks for m in order], axis=1)

    early = list(range(count - TAIL))
    late = list(range(max(count - TAIL, 0), count))
    full_order = x_order + [m ^ 1 for m in x_order]
    sets = {c: (gap_left[:slice_rows], table[:slice_rows], column(right, full_order, [c]), column(key, full_order, [c])) for c in late}
    if early:
        sets[0] = (gap_left, table, column(right, x_order, early), column(key, x_order, early))

    def add_part(left, sides, row_refs, added, outs, name, stream=0):
        arrays = [left, *sides, *row_refs, *added]

        def kernel(*refs):
            part_kernel(*refs, row_count=len(row_refs), added=len(added), stream=stream)

        shapes = [jax.ShapeDtypeStruct((n, aux), PTYPE if i else jnp.float32) for i, n in enumerate(outs)]
        weight = FE if name == "early" else FK
        if stream:
            scratch = [
                pltpu.VMEM((stream, left.shape[0], aux // stream), jnp.float32),
                pltpu.SemaphoreType.DMA((stream,)),
            ]
            return chain.call(kernel, [], arrays, shapes, name, (), weight, ANY, scratch)
        return chain.call(kernel, [], arrays, shapes, name, (), weight)

    far_masks = [half ^ (m * unit) for m in range(places)]
    near_masks = [m * unit for m in range(1, places)]
    group = near_masks + far_masks
    masks, side, got, local, value, wide = {}, {}, {}, {}, {}, {}

    def needed(kind, t):
        label = f"{kind}{t}"
        found = []
        for g, at in FNEED.items():
            if at == label and g in far:
                found += far[g]
        if BNEED == label and beside is not None:
            found.append(beside)
        if kind == XNEED[0] and t - int(XNEED[1]) in wide:
            found += wide[t - int(XNEED[1])]
        if SETNEED == label:
            found += [v for sides in sets.values() for v in sides]
        return found

    def near_of(t, m):
        at, value = [(at, v) for at, v in near[m] if at <= spans[t][0]][-1]
        return value, spans[t][0] - at

    def far_of(t):
        g = [i for i, chunks in enumerate(far_groups) if t in chunks][0]
        return [(v, spans[t][0] - far_spans[g][0]) for v in far[g]]

    def stack_side(t):
        lo, hi = spans[t]
        rows = hi - lo
        parts = [near_of(t, m) for m in range(places - 1)] + far_of(t)
        masks[t] = list(group)
        def kernel(*refs):
            *in_refs, out_ref = refs
            for i, ref in enumerate(in_refs):
                at = parts[i][1]
                out_ref[i * rows : (i + 1) * rows, :] = ref[at : at + rows, :]

        waits = needed("s", t)
        arrays = [v for v, _ in parts]
        out = chain.call(kernel, [], arrays, [block(len(parts) * rows)], f"stack{t}", waits, WS)[0]
        stacked = {0: out}
        for mask in column_masks:
            for m in list(stacked):
                stacked[m ^ mask] = send(stacked[m], "occ", mask)
        side[t] = {col: v for col, v in stacked.items() if col}

    def choose(t):
        lo, hi = spans[t]
        rows = hi - lo
        sources = [(0, turned[0], lo)]
        sources += [(m, v, lo) for m, v in own_side.items()]
        sources += [(m, *near_of(t, i)) for i, m in enumerate(near_masks)]
        sources += [(m, *v) for m, v in zip(far_masks, far_of(t))]
        arrays = [v for _, v, _ in sources]
        for col, v in side[t].items():
            sources += [(m ^ col, len(arrays), i * rows) for i, m in enumerate(masks[t])]
            arrays.append(v)

        def kernel(ids_ref, partner_ref, *refs):
            in_refs, out_refs = refs[: len(arrays)], refs[len(arrays) :]
            for m in range(places):
                for k in range(pairings):
                    here = partner_ref[k, ids_ref[0] ^ (m * unit)] ^ ids_ref[0]
                    for i, (mask, which, at) in enumerate(sources):
                        ref = in_refs[which] if isinstance(which, int) else in_refs[i]

                        @pl.when(here == mask)
                        def _(ref=ref, at=at, k=k, m=m):
                            out_refs[m][k * rows : (k + 1) * rows, :] = ref[at : at + rows, :]

        waits = needed("c", t)
        outs = chain.call(kernel, [ids, partner_list], arrays, [block(pairings * rows)] * places, f"choose{t}", waits, WC)
        local[t] = outs[0]
        got[t] = [send(outs[m], "occ", m * unit) for m in range(1, places)]
        return outs[0]

    def join(t, waits=()):
        rows = spans[t][1] - spans[t][0]
        waits = needed("j", t)

        def kernel(*refs):
            *in_refs, out_ref = refs
            for m, ref in enumerate(in_refs):
                for k in range(pairings):
                    at = (k * places + m) * rows
                    out_ref[at : at + rows, :] = ref[k * rows : (k + 1) * rows, :]

        value[t] = chain.call(
            kernel, [], [local[t], *got[t]], [block(pairings * places * rows)], f"join{t}", waits, WJ
        )[0]
        ready = {0: value[t]}
        mask = virt_count // 2
        while mask > 1:
            for m in list(ready):
                ready[m ^ mask] = send(ready[m], "virt", mask)
            mask //= 2
        wide[t] = [ready[m] for m in x_order]

    added, fulls, held_back = [], {}, []
    def add_early():
        lefts = jnp.concatenate([own, beside], axis=0)
        return add_part(
            lefts, sets[0], [v for c in early for v in wide[c]], [], [slice_rows] + [slice_rows // PCUTS] * PCUTS, "early"
        )

    def full(c):
        if c not in fulls:
            fulls[c] = wide[c] + [send(after(w, *held_back), "virt", 1) for w in wide[c]]
        return fulls[c]

    def gate(kind, t):
        nonlocal beside
        if BSTART == f"{kind}{t}" and early:
            beside = send(after(own, *chain.last), "virt", 1)
        if NGATE == f"{kind}{t}" and NEAR_FIRST < count:
            split = edges[NEAR_FIRST]
            for m in range(1, places):
                near[m - 1].append((split, send(after(turned[m][split:], *chain.last), "occ", m * unit)))
        for g, at in FGATE.items():
            if at == f"{kind}{t}" and g < len(far_groups):
                far[g] = start_far(g, *chain.last)

    beside = None
    for t in range(count):
        steps = [("s", t)] + [("j", t - 1)] * (t > 0)
        if ORDER[t % len(ORDER)] == "j":
            steps = steps[::-1]
        for kind, c in steps:
            (stack_side if kind == "s" else join)(c)
            gate(kind, c)
        if t == count - 1 and EARLY == 0 and early:
            added = add_early()
        choose(t)
        gate("c", t)
    if early and EARLY == 1:
        added = add_early()
    join(count - 1)
    if early and EARLY == 2:
        added = add_early()
    if early:
        held_back = chain.last if CGATE else []
        mine, *others = added
        if PGATE == "j":
            others = [after(v, *chain.last) for v in others]
        added = [mine] + [send(v, "virt", 1) for v in others]
    for c in late:
        stream = STREAM if c == late[-1] else 0
        added = add_part(own, sets[c], full(c), added, [slice_rows], f"late{c}", stream)
    return added[0][None]


def solution(mesh):
    return jax.shard_map(
        body,
        mesh=mesh,
        in_specs=(P("occ", "virt", None), P(), P(), P(), P(None, "occ", "virt", None)),
        out_specs=P("occ", "virt", None),
        check_vma=False,
    )
```
